32 devices in a mesh: gr: 4 (over x, core), gc: 8 (over z, y).
Axes of the slice: x: 2, y: 2, z: 4, core: 2. Of those that a mesh axis runs over, the one named last changes fastest.
Arguments:
- factor_window: bfloat16 [13312, 2048], P('gr', 'gc'), may hold values from -0.125 to 0.125
- upper_panel: bfloat16 [2048, 512], P('gc', 'gr'), may hold values from -6 to 6
- panel_block: float32 [13312, 512], P(('gr', 'gc'))
- first_block: int32 [16], P('gc'), may hold values from 0 to 52
Outputs:
- panel_factor: float32 [13312, 512], P(('gr', 'gc'))
The draws below stay inside these ranges and needn't reach their ends.
All inputs are finite; a program needn't handle non-finite values.
Results may differ from the reference program's by a relative error of at most 0.0003.
Values may be sent and summed in bfloat16 or wider, within the bound.
No kernel may reach another device: no remote copies, remote signals or barrier semaphores. Data moves between devices by JAX's collectives and lax.ppermute only.
A program may use at most 64 MiB of HBM per device.

```python
import math
import jax
import jax.numpy as jnp
from jax import lax

PW = 512
BLK = 128
KC_DEV = 256
MR_DEV = 3328
NS_ITERS = 3
ROWS = 13312
COLS = 2048
N_GR = 4
N_GC = 8


def draw_panel_block(key, part):
    array_shape = (MR_DEV * N_GR, PW)
    entries = jax.random.normal(key, array_shape, jnp.float32)
    row_ids = lax.broadcasted_iota(jnp.int32, array_shape, 0)
    col_ids = lax.broadcasted_iota(jnp.int32, array_shape, 1)
    shift = 6.0 * math.sqrt(PW)
    return entries + jnp.where(row_ids == col_ids, shift, 0.0).astype(jnp.float32)


def draw_first_block(key, part):
    blocks = KC_DEV * N_GC // BLK
    highest = MR_DEV * N_GR // (2 * BLK)
    values = jax.random.randint(jax.random.fold_in(key, 1), (blocks,), 0, highest + 1, dtype=jnp.int32)
    order = jax.random.permutation(jax.random.fold_in(key, 2), blocks)
    values = values.at[order[0]].set(highest)
    values = values.at[order[1]].set(0)
    return values.astype(jnp.int32)


def shard_levels(key, dims, split, low, top_value):
    level = 1.0
    for dim, shards_of in split:
        draws = jax.random.uniform(jax.random.fold_in(jax.random.fold_in(key, 6), dim), (shards_of,), jnp.float32, low / len(split), top_value / len(split))
        level = level * jnp.repeat(jnp.exp(draws), dims[dim] // shards_of).reshape((-1,) + (1,) * (len(dims) - 1 - dim))
    return level


def normal_values(rng, shape, deviation, reach, shards=(), held_as=jnp.bfloat16):
    loudness = shard_levels(rng, shape, shards, -0.22, 0.18) if shards else 1.0
    values = jax.random.normal(rng, shape, jnp.float32) * deviation * loudness
    return jnp.minimum(jnp.maximum(values, -reach), reach).astype(held_as)


def setup_inputs(seed: int = 0) -> dict:
    keys = jax.random.split(jax.random.key(seed), 5)
    factor_window = normal_values(keys[0], (ROWS, COLS), COLS ** -0.5, 0.125, ((0, 4), (1, 8)))
    upper_panel = normal_values(keys[1], (COLS, PW), 1.0, 6.0, ((0, 8), (1, 4)))
    panel_block = draw_panel_block(jax.random.fold_in(keys[4], 71), 0)
    first_block = draw_first_block(jax.random.fold_in(keys[4], 71), 0)
    return dict(factor_window=factor_window, upper_panel=upper_panel, panel_block=panel_block, first_block=first_block)


def masked_rows(slab_block, slab_start, col_first):
    row_ids = slab_start + jnp.arange(slab_block.shape[0], dtype=jnp.int32)
    inside = (row_ids // BLK)[:, None] >= col_first[None, :]
    return jnp.where(inside, slab_block, jnp.zeros_like(slab_block))


def reference(factor_window, upper_panel, panel_block, first_block):
    col_first = jnp.repeat(first_block, BLK)
    slabs = factor_window.reshape(N_GR, MR_DEV, KC_DEV * N_GC)
    starts = jnp.arange(N_GR, dtype=jnp.int32) * MR_DEV

    def slab_product(slab_item):
        slab_block, slab_start = slab_item
        return jnp.dot(masked_rows(slab_block, slab_start, col_first), upper_panel, preferred_element_type=jnp.float32)

    update = lax.map(slab_product, (slabs, starts)).reshape(N_GR * MR_DEV, PW)
    schur_rows = panel_block - update
    pivot_block = schur_rows[:PW]
    pivot_scale = jnp.mean(jnp.diagonal(pivot_block))
    scaled = pivot_block / pivot_scale
    inverse = jnp.eye(PW, dtype=jnp.float32)
    for iteration in range(NS_ITERS):
        partial_value = jnp.dot(scaled, inverse, precision=lax.Precision.HIGHEST)
        inverse = 2.0 * inverse - jnp.dot(inverse, partial_value, precision=lax.Precision.HIGHEST)
    factor = jnp.dot(schur_rows, inverse, precision=lax.Precision.HIGHEST) / pivot_scale
    return factor.at[:PW].set(inverse)
```

```python
import jax
import jax.numpy as jnp
from jax import lax
from jax.sharding import PartitionSpec as P

BLK = 128
NS_ITERS = 3
CORES = 2
WIRE = jnp.float16


def inner_size(n):
    return max(d for d in range(1, n + 1) if n % d == 0 and d * d <= n)


class Grid:
    def __init__(self):
        self.gr = lax.axis_size("gr")
        self.gc = lax.axis_size("gc")
        self.cores = CORES if self.gr % CORES == 0 else 1
        self.xs = self.gr // self.cores
        self.ys = inner_size(self.gc)
        self.zs = self.gc // self.ys
        gr, gc = lax.axis_index("gr"), lax.axis_index("gc")
        self.x, self.core = gr // self.cores, gr % self.cores
        self.z, self.y = gc // self.ys, gc % self.ys
        self.gr_index, self.gc_index = gr, gc

    def swap(self, value, dx=0, dcore=0, dz=0, dy=0, sources=None):
        pairs = []
        for gr in range(self.gr):
            for gc in range(self.gc):
                if sources is not None and not sources(gr, gc):
                    continue
                to_gr = ((gr // self.cores) ^ dx) * self.cores + ((gr % self.cores) ^ dcore)
                to_gc = ((gc // self.ys) ^ dz) * self.ys + ((gc % self.ys) ^ dy)
                pairs.append((gr * self.gc + gc, to_gr * self.gc + to_gc))
        return lax.ppermute(value, ("gr", "gc"), pairs)


def rows_of(value, start, count):
    return lax.dynamic_slice_in_dim(value, start, count, axis=0)


def body(factor_window, upper_panel, panel_block, first_block):
    grid = Grid()
    local_rows, depth = factor_window.shape
    own_rows, panel_width = panel_block.shape
    row_base = grid.gr_index * local_rows
    col_first = jnp.repeat(first_block, BLK)
    global_start = (grid.gr_index * grid.gc + grid.gc_index) * own_rows

    def masked(start, count):
        row_ids = row_base + start + jnp.arange(count, dtype=jnp.int32)
        inside = (row_ids // BLK)[:, None] >= col_first[None, :]
        part = rows_of(factor_window, start, count)
        return jnp.where(inside, part, jnp.zeros_like(part))

    def chunk(k, j):
        return masked(((grid.z ^ k) * grid.ys + (grid.y ^ j)) * own_rows, own_rows)

    plane = [(a, b) for b in range(grid.ys) for a in range(grid.xs)]
    piece = panel_width // (grid.gr * grid.ys)
    chip_rows = piece * grid.cores

    def chip_start(x, y):
        return (y * grid.xs + x) * chip_rows

    shards, pivot_rows = {}, {}
    halves = depth // upper_panel.shape[1]
    for a, b in plane:
        rows = masked(chip_start(grid.x ^ a, grid.y ^ b), chip_rows)
        if (a, b) == (0, 0):
            shards[a, b], pivot_rows[a, b] = upper_panel, rows
            continue
        packed = jnp.concatenate([upper_panel] + jnp.split(rows, halves, axis=1), axis=0)
        packed = grid.swap(packed, dx=a, dy=b)
        shards[a, b] = packed[:depth]
        pivot_rows[a, b] = jnp.concatenate(jnp.split(packed[depth:], halves, axis=0), axis=1)
    picked = []
    for b in range(grid.ys):
        stack = jnp.stack([pivot_rows[a, b] for a in range(grid.xs)])
        picked.append(lax.dynamic_index_in_dim(stack, grid.x, 0, keepdims=False))
    picked = jnp.concatenate(picked, axis=1)
    shard_stack = jnp.stack([shards[a, b] for a, b in plane])
    other_stack = grid.swap(shard_stack, dcore=1) if grid.cores > 1 else None

    def panel_columns(b):
        blocks = []
        for gr in range(grid.gr):
            x, core = gr // grid.cores, gr % grid.cores
            index = b * grid.xs + (grid.x ^ x)
            mine = lax.dynamic_index_in_dim(shard_stack, index, 0, keepdims=False)
            if other_stack is not None:
                theirs = lax.dynamic_index_in_dim(other_stack, index, 0, keepdims=False)
                mine = jnp.where(grid.core == core, mine, theirs)
            blocks.append(mine)
        return jnp.concatenate(blocks, axis=1)

    panel = jnp.concatenate([panel_columns(b) for b in range(grid.ys)], axis=0)
    if grid.cores > 1:
        others = grid.swap(rows_of(picked, piece, piece), dcore=1, sources=lambda gr, gc: gr == 0 or gr % grid.cores == 0)
        pivot_part = jnp.where(grid.core == 0, picked[:piece], others)
    else:
        pivot_part = picked

    def holds(gr, gc):
        return gr == 0 and gc * own_rows < panel_width

    padded = jnp.zeros((panel_width + own_rows, panel_width), jnp.float32)
    padded = lax.dynamic_update_slice_in_dim(padded, panel_block, jnp.minimum(global_start, panel_width), axis=0)
    before = None
    for a, b in plane:
        rows = rows_of(padded, chip_start(grid.x ^ a, grid.y ^ b), chip_rows)
        if (a, b) == (0, 0):
            rows = jnp.where(grid.gr_index == 0, rows, 0.0)
        else:
            rows = grid.swap(rows, dx=a, dy=b, sources=holds)
        before = rows if before is None else before + rows
    if grid.cores > 1:
        others = grid.swap(before[piece:], dcore=1, sources=lambda gr, gc: gr % grid.cores == 0)
        before = jnp.where(grid.core == 0, before[:piece], others)

    total = before - jnp.dot(pivot_part, panel, preferred_element_type=jnp.float32)
    step = 1
    while step < grid.zs:
        total = total + grid.swap(total, dz=step)
        step *= 2
    pieces = {(0, 0): total}
    for a, b in plane[1:]:
        pieces[a, b] = grid.swap(total, dx=a, dy=b)
    piece_stack = jnp.stack([pieces[a, b] for a, b in plane])
    other_pieces = grid.swap(piece_stack, dcore=1) if grid.cores > 1 else None
    blocks = []
    for y in range(grid.ys):
        for x in range(grid.xs):
            index = (grid.y ^ y) * grid.xs + (grid.x ^ x)
            mine = lax.dynamic_index_in_dim(piece_stack, index, 0, keepdims=False)
            if other_pieces is None:
                blocks.append(mine)
                continue
            theirs = lax.dynamic_index_in_dim(other_pieces, index, 0, keepdims=False)
            for core in range(grid.cores):
                blocks.append(jnp.where(grid.core == core, mine, theirs))
    pivot_block = jnp.concatenate(blocks, axis=0)

    order = list(range(grid.zs - 1, -1, -1))
    arrived = {}
    for ks in ([order[0]], order[1:]):
        if not ks:
            continue
        for j in range(1, grid.ys):
            got = grid.swap(jnp.concatenate([chunk(k, j) for k in ks], axis=0), dy=j)
            for n, k in enumerate(ks):
                arrived[k, j] = got[n * own_rows : (n + 1) * own_rows]
    sums = {}
    for k in order:
        whole = jnp.concatenate([chunk(k, 0)] + [arrived[k, j] for j in range(1, grid.ys)], axis=1)
        sums[k] = jnp.dot(whole, panel, preferred_element_type=jnp.float32)
    step = 1
    while step < grid.zs:
        for k in sorted((k for k in sums if k & step), reverse=True):
            got = grid.swap(sums.pop(k).astype(WIRE), dz=step)
            sums[k ^ step] = sums[k ^ step] + got.astype(jnp.float32)
        step *= 2
    schur_rows = panel_block - sums[0]

    pivot_scale = jnp.mean(jnp.diagonal(pivot_block))
    scaled = pivot_block / pivot_scale
    eye = jnp.eye(panel_width, dtype=jnp.float32)
    inverse = 2.0 * eye - scaled
    for iteration in range(NS_ITERS - 1):
        partial_value = jnp.dot(scaled, inverse, precision=lax.Precision.HIGHEST)
        inverse = 2.0 * inverse - jnp.dot(inverse, partial_value, precision=lax.Precision.HIGHEST)
    factor = jnp.dot(schur_rows, inverse, precision=lax.Precision.HIGHEST) / pivot_scale
    tail = jnp.pad(inverse, ((0, own_rows), (0, 0)))
    from_inverse = rows_of(tail, jnp.minimum(global_start, panel_width), own_rows)
    rows_global = global_start + jnp.arange(own_rows, dtype=jnp.int32)
    return jnp.where((rows_global < panel_width)[:, None], from_inverse, factor)


def solution(mesh):
    return jax.shard_map(
        body,
        mesh=mesh,
        in_specs=(P("gr", "gc"), P("gc", "gr"), P(("gr", "gc"), None), P("gc")),
        out_specs=P(("gr", "gc"), None),
        check_vma=False,
    )
```

```python
import functools

import jax
import jax.numpy as jnp
from jax import lax
from jax.experimental import pallas as pl
from jax.experimental.pallas import tpu as pltpu
from jax.sharding import PartitionSpec as P

BLK = 128
NS_ITERS = 3
CORES = 2
WIRE = jnp.float16
LANES = 128
ROW_TILE = 16
VMEM = pl.BlockSpec(memory_space=pltpu.VMEM)
SMEM = pl.BlockSpec(memory_space=pltpu.SMEM)
PARAMS = pltpu.CompilerParams(vmem_limit_bytes=40 * 2**20)


def inner_size(n):
    return max(d for d in range(1, n + 1) if n % d == 0 and d * d <= n)


class Grid:
    def __init__(self):
        self.gr = lax.axis_size("gr")
        self.gc = lax.axis_size("gc")
        self.cores = CORES if self.gr % CORES == 0 else 1
        self.xs = self.gr // self.cores
        self.ys = inner_size(self.gc)
        self.zs = self.gc // self.ys
        gr, gc = lax.axis_index("gr"), lax.axis_index("gc")
        self.x, self.core = gr // self.cores, gr % self.cores
        self.z, self.y = gc // self.ys, gc % self.ys
        self.gr_index, self.gc_index = gr, gc
        self.plane = [(a, b) for b in range(self.ys) for a in range(self.xs)]

    def swap(self, value, dx=0, dcore=0, dz=0, dy=0, sources=None):
        pairs = []
        for gr in range(self.gr):
            for gc in range(self.gc):
                if sources is not None and not sources(gr, gc):
                    continue
                to_gr = ((gr // self.cores) ^ dx) * self.cores + ((gr % self.cores) ^ dcore)
                to_gc = ((gc // self.ys) ^ dz) * self.ys + ((gc % self.ys) ^ dy)
                pairs.append((gr * self.gc + gc, to_gr * self.gc + to_gc))
        return lax.ppermute(value, ("gr", "gc"), pairs)


def rows_of(value, start, count):
    return lax.dynamic_slice_in_dim(value, start, count, axis=0)


def shape(rows, columns, dtype):
    return jax.ShapeDtypeStruct((rows, columns), dtype)


def below_skyline(part, first_row, first_of):
    row_ids = first_row + lax.broadcasted_iota(jnp.int32, (part.shape[0], 1), 0)
    kept = []
    for c in range(part.shape[1] // BLK):
        block = part[:, c * BLK : (c + 1) * BLK]
        kept.append(jnp.where(row_ids >= first_of(c) * BLK, block, jnp.zeros_like(block)))
    return jnp.concatenate(kept, axis=1)


def chunks_kernel(indices, base, first, window_ref, out_ref):
    rows = out_ref.shape[0]
    start = base[0] + indices[pl.program_id(0)] * rows
    out_ref[...] = below_skyline(window_ref[...], start, lambda c: first[c])


def masked_chunks(window, first_block, row_base, indices, rows):
    depth = window.shape[1]
    count = indices.shape[0]
    return pl.pallas_call(
        chunks_kernel,
        grid_spec=pltpu.PrefetchScalarGridSpec(
            num_scalar_prefetch=3,
            grid=(count,),
            in_specs=[pl.BlockSpec((rows, depth), lambda i, indices, base, first: (indices[i], 0))],
            out_specs=pl.BlockSpec((rows, depth), lambda i, indices, base, first: (i, 0)),
        ),
        out_shape=shape(count * rows, depth, window.dtype),
        cost_estimate=pl.CostEstimate(flops=0, bytes_accessed=4 * count * rows * depth, transcendentals=0),
        name="masked_chunks",
    )(indices, row_base[None], first_block, window)


def front_kernel(chip_rows, targets, starts, base, first, panel_ref, head_ref, *out_refs):
    depth, width = panel_ref.shape
    for n in range(targets):
        start = pl.multiple_of(starts[n], chip_rows)
        rows = below_skyline(head_ref[pl.ds(start, chip_rows), :], base[0] + start, lambda c: first[c])
        if n == 0:
            out_refs[0][...] = rows
            continue
        out_refs[n][:depth, :] = panel_ref[...]
        for h in range(depth // width):
            out_refs[n][depth + h * chip_rows : depth + (h + 1) * chip_rows, :] = rows[:, h * width : (h + 1) * width]


def front_pack(upper_panel, head, first_block, row_base, starts, chip_rows):
    depth, width = upper_panel.shape
    targets = starts.shape[0]
    packed = shape(depth + chip_rows * depth // width, width, head.dtype)
    return pl.pallas_call(
        functools.partial(front_kernel, chip_rows, targets),
        in_specs=[SMEM, SMEM, SMEM, VMEM, pl.BlockSpec(head.shape, lambda: (0, 0))],
        out_specs=[VMEM] * targets,
        out_shape=[shape(chip_rows, depth, head.dtype)] + [packed] * (targets - 1),
        name="front_pack",
    )(starts, row_base[None], first_block, upper_panel, head)


def chip_kernel(xs, ys, cores, place, panel_ref, rows_ref, *refs):
    arrived, (out_ref, mine_ref) = refs[:-2], refs[-2:]
    depth, width = panel_ref.shape
    chip_rows = rows_ref.shape[0]
    piece = chip_rows // cores
    halves = depth // width
    x = place[0]
    base = xs * ys * depth
    for b in range(ys):
        picked = [jnp.zeros((chip_rows, width), rows_ref.dtype)] * halves
        for a in range(xs):
            n = b * xs + a
            if n == 0:
                out_ref[:depth, :] = panel_ref[...]
                found = [rows_ref[:, h * width : (h + 1) * width] for h in range(halves)]
            else:
                got = arrived[n - 1]
                out_ref[n * depth : (n + 1) * depth, :] = got[:depth, :]
                found = [got[depth + h * chip_rows : depth + (h + 1) * chip_rows, :] for h in range(halves)]
            picked = [jnp.where(x == a, new, old) for new, old in zip(found, picked)]
        for h in range(halves):
            n = b * halves + h
            mine_ref[:, n * width : (n + 1) * width] = picked[h][:piece]
            if cores > 1:
                out_ref[base + n * piece : base + (n + 1) * piece, :] = picked[h][piece:]


def chip_pack(grid, place, upper_panel, own_rows, arrived):
    depth, width = upper_panel.shape
    chip_rows = own_rows.shape[0]
    piece = chip_rows // grid.cores
    span = grid.ys * depth
    rows = len(grid.plane) * depth + span // width * piece
    return pl.pallas_call(
        functools.partial(chip_kernel, grid.xs, grid.ys, grid.cores),
        in_specs=[SMEM] + [VMEM] * (2 + len(arrived)),
        out_specs=[VMEM, VMEM],
        out_shape=[shape(rows, width, upper_panel.dtype), shape(piece, span, upper_panel.dtype)],
        name="chip_pack",
    )(place, upper_panel, own_rows, *arrived)


def panel_kernel(xs, ys, cores, depth, place, rows_ref, *refs):
    packs, (panel_ref, update_ref) = refs[:-2], refs[-2:]
    width = packs[0].shape[1]
    piece = rows_ref.shape[0]
    x, core = place[0], place[1]
    for b in range(ys):
        for a in range(xs):
            n = b * xs + a
            for e in range(cores):
                gr = jnp.bitwise_xor(x, a) * cores + jnp.bitwise_xor(core, e)
                columns = pl.ds(pl.multiple_of(gr * width, width), width)
                panel_ref[b * depth : (b + 1) * depth, columns] = packs[e][n * depth : (n + 1) * depth, :]
    rows = rows_ref[...]
    if cores > 1:
        base = xs * ys * depth
        count = rows.shape[1] // width
        theirs = [packs[1][base + n * piece : base + (n + 1) * piece, :] for n in range(count)]
        rows = jnp.where(core == 0, rows, jnp.concatenate(theirs, axis=1))
    update_ref[...] = jnp.dot(rows, panel_ref[...], preferred_element_type=jnp.float32)


def panel_assemble(grid, place, depth, rows, packs):
    width = packs[0].shape[1]
    total = grid.gr * width
    return pl.pallas_call(
        functools.partial(panel_kernel, grid.xs, grid.ys, grid.cores, depth),
        in_specs=[SMEM] + [VMEM] * (1 + len(packs)),
        out_specs=[VMEM, VMEM],
        out_shape=[shape(grid.ys * depth, total, rows.dtype), shape(rows.shape[0], total, jnp.float32)],
        name="panel_assemble",
    )(place, rows, *packs)


def two_parts(value):
    high = value.astype(jnp.bfloat16)
    return high, (value - high.astype(jnp.float32)).astype(jnp.bfloat16)


def product(left, right):
    dot = functools.partial(jnp.dot, preferred_element_type=jnp.float32)
    return dot(left[0], right[0]) + (dot(left[0], right[1]) + dot(left[1], right[0]))


def inverse_kernel(xs, ys, cores, place, *refs):
    stacks, (high_ref, low_ref, scale_ref, pivot_ref) = refs[:cores], refs[cores:]
    piece = stacks[0].shape[0] // (xs * ys)
    x, core, y = place[0], place[1], place[2]
    for b in range(ys):
        for a in range(xs):
            n = b * xs + a
            chip = jnp.bitwise_xor(y, b) * xs + jnp.bitwise_xor(x, a)
            for e in range(cores):
                start = (chip * cores + jnp.bitwise_xor(core, e)) * piece
                pivot_ref[pl.ds(pl.multiple_of(start, piece), piece), :] = stacks[e][n * piece : (n + 1) * piece, :]
    order = pivot_ref.shape[0]
    square = (order, order)
    diagonal = lax.broadcasted_iota(jnp.int32, square, 0) == lax.broadcasted_iota(jnp.int32, square, 1)
    pivot = pivot_ref[...]
    scale = jnp.sum(jnp.where(diagonal, pivot, 0.0)) / order
    power = jnp.where(diagonal, 1.0, 0.0) - pivot / scale
    rest = power
    parts = two_parts(power)
    for step in range(NS_ITERS - 1):
        power = product(parts, parts)
        parts = two_parts(power)
        rest = rest + power + product(two_parts(rest), parts)
    high_ref[...], low_ref[...] = two_parts(rest)
    scale_ref[0] = scale


def inverse_rest(grid, place, stacks):
    order = stacks[0].shape[1]
    half = shape(order, order, jnp.bfloat16)
    return pl.pallas_call(
        functools.partial(inverse_kernel, grid.xs, grid.ys, grid.cores),
        in_specs=[SMEM] + [VMEM] * len(stacks),
        out_specs=[VMEM, VMEM, SMEM],
        out_shape=[half, half, jax.ShapeDtypeStruct((1,), jnp.float32)],
        scratch_shapes=[pltpu.VMEM((order, order), jnp.float32)],
        compiler_params=PARAMS,
        cost_estimate=pl.CostEstimate(flops=24 * order**3, bytes_accessed=8 * order**2, transcendentals=0),
        name="pivot_inverse",
    )(place, *stacks)


def factor_kernel(start_ref, scale_ref, schur_ref, high_ref, low_ref, out_ref):
    rows, order = out_ref.shape
    schur = schur_ref[...]
    rest = high_ref[...], low_ref[...]
    out_ref[...] = (schur + product(two_parts(schur), rest)) / scale_ref[0]
    start = start_ref[0]

    @pl.when(start < order)
    def _():
        here = start + lax.broadcasted_iota(jnp.int32, (rows, order), 0)
        across = lax.broadcasted_iota(jnp.int32, (rows, order), 1)
        pick = jnp.where(here == across, 1.0, 0.0).astype(jnp.bfloat16)
        dot = functools.partial(jnp.dot, preferred_element_type=jnp.float32)
        inverse = pick.astype(jnp.float32) + (dot(pick, rest[0]) + dot(pick, rest[1]))
        out_ref[...] = jnp.where(here < order, inverse, out_ref[...])


def factor_rows(global_start, scale, schur, high, low):
    rows, order = schur.shape
    return pl.pallas_call(
        factor_kernel,
        in_specs=[SMEM, SMEM, VMEM, VMEM, VMEM],
        out_specs=VMEM,
        out_shape=shape(rows, order, jnp.float32),
        compiler_params=PARAMS,
        name="factor_rows",
    )(global_start[None], scale, schur, high, low)


def masked_rows(window, first_block, row_base, start, count):
    col_first = jnp.repeat(first_block, BLK)
    row_ids = row_base + start + jnp.arange(count, dtype=jnp.int32)
    inside = (row_ids // BLK)[:, None] >= col_first[None, :]
    part = rows_of(window, start, count)
    return jnp.where(inside, part, jnp.zeros_like(part))


def plain_front_pack(upper_panel, head, first_block, row_base, starts, chip_rows):
    depth, width = upper_panel.shape
    out = []
    for n in range(starts.shape[0]):
        rows = masked_rows(head, first_block, row_base, starts[n], chip_rows)
        out.append(rows if n == 0 else jnp.concatenate([upper_panel] + jnp.split(rows, depth // width, axis=1), axis=0))
    return out


def plain_chip_pack(grid, place, upper_panel, own_rows, arrived):
    depth, width = upper_panel.shape
    chip_rows = own_rows.shape[0]
    piece = chip_rows // grid.cores
    halves = depth // width
    rows = [jnp.concatenate(jnp.split(own_rows, halves, axis=1), axis=0)] + [got[depth:] for got in arrived]
    shards = [upper_panel] + [got[:depth] for got in arrived]
    mine, theirs = [], []
    for b in range(grid.ys):
        stack = jnp.stack(rows[b * grid.xs : (b + 1) * grid.xs])
        picked = lax.dynamic_index_in_dim(stack, grid.x, 0, keepdims=False).reshape(halves, chip_rows, width)
        mine += [picked[h, :piece] for h in range(halves)]
        theirs += [picked[h, piece:] for h in range(halves)]
    return jnp.concatenate(shards + theirs, axis=0), jnp.concatenate(mine, axis=1)


def plain_panel_assemble(grid, place, depth, rows, packs):
    width = packs[0].shape[1]
    count = len(grid.plane)
    stack = jnp.stack([pack[: count * depth].reshape(count, depth, width) for pack in packs])
    bands = []
    for b in range(grid.ys):
        bands.append(
            jnp.concatenate(
                [stack[grid.core ^ (gr % grid.cores), b * grid.xs + (grid.x ^ (gr // grid.cores))] for gr in range(grid.gr)], axis=1
            )
        )
    panel = jnp.concatenate(bands, axis=0)
    if grid.cores > 1:
        theirs = packs[1][count * depth :].reshape(-1, rows.shape[0], width)
        rows = jnp.where(grid.core == 0, rows, jnp.concatenate(list(theirs), axis=1))
    return panel, jnp.dot(rows, panel, preferred_element_type=jnp.float32)


def body(factor_window, upper_panel, panel_block, first_block):
    grid = Grid()
    local_rows, depth = factor_window.shape
    own_rows, panel_width = panel_block.shape
    width = upper_panel.shape[1]
    row_base = grid.gr_index * local_rows
    global_start = (grid.gr_index * grid.gc + grid.gc_index) * own_rows
    place = jnp.stack([grid.x, grid.core, grid.y])
    piece = panel_width // (grid.gr * grid.ys)
    chip_rows = piece * grid.cores
    whole_tiles = width % LANES == 0 and piece % ROW_TILE == 0
    whole_chunks = own_rows % ROW_TILE == 0

    def chip_start(a, b):
        return ((grid.y ^ b) * grid.xs + (grid.x ^ a)) * chip_rows

    starts = jnp.stack([chip_start(a, b) for a, b in grid.plane])
    head = factor_window[:panel_width]
    steps = (front_pack, chip_pack, panel_assemble) if whole_tiles else (plain_front_pack, plain_chip_pack, plain_panel_assemble)

    own_pivot, *packed = steps[0](upper_panel, head, first_block, row_base, starts, chip_rows)
    arrived = [grid.swap(pack, dx=a, dy=b) for pack, (a, b) in zip(packed, grid.plane[1:])]

    order = list(range(grid.zs - 1, -1, -1))

    def chunks(ks, j):
        indices = jnp.stack([(grid.z ^ k) * grid.ys + (grid.y ^ j) for k in ks])
        if whole_chunks:
            return masked_chunks(factor_window, first_block, row_base, indices, own_rows)
        parts = [masked_rows(factor_window, first_block, row_base, i * own_rows, own_rows) for i in indices]
        return jnp.concatenate(parts, axis=0)

    columns = {}
    for ks in ([order[0]], order[1:]):
        if not ks:
            continue
        bands = [grid.swap(chunks(ks, j), dy=j) for j in range(1, grid.ys)]
        bands = [chunks(ks, 0)] + bands
        for n, k in enumerate(ks):
            columns[k] = [band[n * own_rows : (n + 1) * own_rows] for band in bands]

    pack, mine = steps[1](grid, place, upper_panel, own_pivot, arrived)
    packs = [pack] + ([grid.swap(pack, dcore=1)] if grid.cores > 1 else [])
    panel, pivot_update = steps[2](grid, place, depth, mine, packs)

    def holds(gr, gc):
        return gr == 0 and gc * own_rows < panel_width

    padded = jnp.zeros((panel_width + own_rows, panel_width), jnp.float32)
    padded = lax.dynamic_update_slice_in_dim(padded, panel_block, jnp.minimum(global_start, panel_width), axis=0)
    before = jnp.where(grid.gr_index == 0, rows_of(padded, starts[0], chip_rows), 0.0)
    for n, (a, b) in enumerate(grid.plane):
        if n:
            before = before + grid.swap(rows_of(padded, starts[n], chip_rows), dx=a, dy=b, sources=holds)
    if grid.cores > 1:
        others = grid.swap(before[piece:], dcore=1, sources=lambda gr, gc: gr % grid.cores == 0)
        before = jnp.where(grid.core == 0, before[:piece], others)

    total = before - pivot_update
    step = 1
    while step < grid.zs:
        total = total + grid.swap(total, dz=step)
        step *= 2
    stack = jnp.concatenate([total] + [grid.swap(total, dx=a, dy=b) for a, b in grid.plane[1:]], axis=0)
    stacks = [stack] + ([grid.swap(stack, dcore=1)] if grid.cores > 1 else [])
    high, low, scale = inverse_rest(grid, place, stacks)

    sums = {}
    for k in order:
        bands = [panel[j * depth : (j + 1) * depth] for j in range(grid.ys)]
        parts = [jnp.dot(part, band, preferred_element_type=jnp.float32) for part, band in zip(columns[k], bands)]
        sums[k] = sum(parts[1:], parts[0])
    step = 1
    while step < grid.zs:
        for k in sorted((k for k in sums if k & step), reverse=True):
            got = grid.swap(sums.pop(k).astype(WIRE), dz=step)
            sums[k ^ step] = sums[k ^ step] + got.astype(jnp.float32)
        step *= 2
    schur_rows = panel_block - sums[0]
    return factor_rows(global_start, scale, schur_rows, high, low)


def solution(mesh):
    return jax.shard_map(
        body,
        mesh=mesh,
        in_specs=(P("gr", "gc"), P("gc", "gr"), P(("gr", "gc"), None), P("gc")),
        out_specs=P(("gr", "gc"), None),
        check_vma=False,
    )
```

```python
import functools

import jax
import jax.numpy as jnp
from jax import lax
from jax.experimental import pallas as pl
from jax.experimental.pallas import tpu as pltpu
from jax.sharding import PartitionSpec as P

BLK = 128
NS_ITERS = 3
CORES = 2
WIRE = jnp.float16
LANES = 128
ROW_TILE = 16
VMEM = pl.BlockSpec(memory_space=pltpu.VMEM)
SMEM = pl.BlockSpec(memory_space=pltpu.SMEM)
HBM = pl.BlockSpec(memory_space=pltpu.HBM)
QUICK = pl.CostEstimate(flops=0, bytes_accessed=0, transcendentals=0)
PARAMS = pltpu.CompilerParams(vmem_limit_bytes=12 * 2**20)


def inner_size(n):
    return max(d for d in range(1, n + 1) if n % d == 0 and d * d <= n)


class Grid:
    def __init__(self):
        self.gr = lax.axis_size("gr")
        self.gc = lax.axis_size("gc")
        self.cores = CORES if self.gr % CORES == 0 else 1
        self.xs = self.gr // self.cores
        self.ys = inner_size(self.gc)
        self.zs = self.gc // self.ys
        gr, gc = lax.axis_index("gr"), lax.axis_index("gc")
        self.x, self.core = gr // self.cores, gr % self.cores
        self.z, self.y = gc // self.ys, gc % self.ys
        self.gr_index, self.gc_index = gr, gc
        self.plane = [(a, b) for b in range(self.ys) for a in range(self.xs)]

    def swap(self, value, dx=0, dcore=0, dz=0, dy=0):
        return self.permute(value, lambda core: (dx, dcore, dz, dy))

    def permute(self, value, moves):
        pairs = []
        for gr in range(self.gr):
            for gc in range(self.gc):
                core = gr % self.cores
                dx, dcore, dz, dy = moves(core)
                to_gr = ((gr // self.cores) ^ dx) * self.cores + (core ^ dcore)
                to_gc = ((gc // self.ys) ^ dz) * self.ys + ((gc % self.ys) ^ dy)
                pairs.append((gr * self.gc + gc, to_gr * self.gc + to_gc))
        return lax.ppermute(value, ("gr", "gc"), pairs)


def rows_of(value, start, count):
    return lax.dynamic_slice_in_dim(value, start, count, axis=0)


def shape(rows, columns, dtype):
    return pltpu.VMEM((rows, columns), dtype)


def placed(space, *values):
    return [pltpu.with_memory_space_constraint(value, space) for value in values]


def below_skyline(part, first_row, first_of):
    row_ids = first_row + lax.broadcasted_iota(jnp.int32, (part.shape[0], 1), 0)
    kept = []
    for c in range(part.shape[1] // BLK):
        block = part[:, c * BLK : (c + 1) * BLK]
        kept.append(jnp.where(row_ids >= first_of(c) * BLK, block, jnp.zeros_like(block)))
    return jnp.concatenate(kept, axis=1)


def chunks_kernel(ys, ks, j, own_rows, first, window_ref, *refs):
    shard_refs, (out_ref, sems) = refs[:-2], refs[-2:]
    gr, gc = lax.axis_index("gr"), lax.axis_index("gc")
    z, y = gc // ys, gc % ys
    base = gr * window_ref.shape[0]
    starts = [(jnp.bitwise_xor(z, k) * ys + jnp.bitwise_xor(y, j)) * own_rows for k in ks]
    places = [pl.ds(n * own_rows, own_rows) for n in range(len(ks))]
    copies = [
        pltpu.make_async_copy(
            window_ref.at[pl.ds(pl.multiple_of(start, ROW_TILE), own_rows), :], out_ref.at[place, :], sems.at[n]
        )
        for n, (start, place) in enumerate(zip(starts, places))
    ]
    for copy in copies:
        copy.start()
    for shard in shard_refs:
        out_ref[len(ks) * own_rows :, :] = across(shard[...], out_ref.shape[1])
    for copy, start, place in zip(copies, starts, places):
        copy.wait()
        out_ref[place, :] = below_skyline(out_ref[place, :], base + start, lambda c: first[c])


def across(shard, columns):
    return jnp.concatenate(jnp.split(shard, columns // shard.shape[1], axis=0), axis=1)


def masked_chunks(grid, window, first_block, ks, j, own_rows, *shard):
    extra = sum(part.size // window.shape[1] for part in shard)
    return pl.pallas_call(
        functools.partial(chunks_kernel, grid.ys, ks, j, own_rows),
        in_specs=[SMEM, HBM] + [VMEM] * len(shard),
        out_specs=VMEM,
        out_shape=shape(len(ks) * own_rows + extra, window.shape[1], window.dtype),
        scratch_shapes=[pltpu.SemaphoreType.DMA((len(ks),))],
        compiler_params=PARAMS,
        cost_estimate=QUICK,
        name="masked_chunks",
    )(first_block, *placed(pltpu.HBM, window), *shard)


def plain_masked_chunks(grid, window, first_block, ks, j, own_rows, *shard):
    parts = []
    for k in ks:
        start = ((grid.z ^ k) * grid.ys + (grid.y ^ j)) * own_rows
        parts.append(masked_rows(rows_of(window, start, own_rows), first_block, grid.gr_index * window.shape[0] + start))
    return jnp.concatenate(parts + [across(part, window.shape[1]) for part in shard], axis=0)


def pivot_pack_kernel(xs, ys, cores, first, window_ref, block_ref, *refs):
    out_refs, (head, padded, head_sem, block_sem) = refs[:-4], refs[-4:]
    chip_rows = out_refs[0].shape[0]
    own_rows, order = block_ref.shape
    depth = head.shape[1]
    gr, gc = lax.axis_index("gr"), lax.axis_index("gc")
    x, y = gr // cores, gc % ys
    begin = gc * own_rows
    head_copy = pltpu.make_async_copy(window_ref.at[pl.ds(0, order), :], head, head_sem)
    block_copy = pltpu.make_async_copy(block_ref, padded.at[pl.ds(chip_rows, own_rows), :], block_sem)
    holds = (gr == 0) & (begin < order)

    def start_of(n):
        return (jnp.bitwise_xor(y, n // xs) * xs + jnp.bitwise_xor(x, n % xs)) * chip_rows

    @pl.when(gr == 0)
    def _():
        head_copy.start()

    @pl.when(holds)
    def _():
        block_copy.start()

    for out_ref in out_refs:
        out_ref[...] = jnp.zeros_like(out_ref)

    @pl.when(gr == 0)
    def _():
        head_copy.wait()
        for n, out_ref in enumerate(out_refs):
            rows = head[pl.ds(pl.multiple_of(start_of(n), chip_rows), chip_rows), :]
            out_ref[:, :depth] = below_skyline(rows, start_of(n), lambda c: first[c])

    @pl.when(holds)
    def _():
        edge = jnp.zeros((chip_rows, order), jnp.float32)
        padded[:chip_rows, :] = edge
        padded[chip_rows + own_rows :, :] = edge
        block_copy.wait()
        for n, out_ref in enumerate(out_refs):
            place = jnp.clip(start_of(n) - begin + chip_rows, 0, chip_rows + own_rows)
            high, low = two_parts(padded[pl.ds(pl.multiple_of(place, 8), chip_rows), :])
            out_ref[:, depth : depth + order] = high
            out_ref[:, depth + order :] = low


def pivot_pack(grid, window, panel_block, first_block, chip_rows):
    own_rows, order = panel_block.shape
    depth = window.shape[1]
    targets = len(grid.plane)
    return pl.pallas_call(
        functools.partial(pivot_pack_kernel, grid.xs, grid.ys, grid.cores),
        in_specs=[SMEM, HBM, HBM],
        out_specs=[VMEM] * targets,
        out_shape=[shape(chip_rows, depth + 2 * order, window.dtype)] * targets,
        scratch_shapes=[
            pltpu.VMEM((order, depth), window.dtype),
            pltpu.VMEM((own_rows + 2 * chip_rows, order), jnp.float32),
            pltpu.SemaphoreType.DMA,
            pltpu.SemaphoreType.DMA,
        ],
        compiler_params=PARAMS,
        cost_estimate=QUICK,
        name="pivot_pack",
    )(first_block, *placed(pltpu.HBM, window, panel_block))


def plain_pivot_pack(grid, window, panel_block, first_block, chip_rows):
    own_rows, order = panel_block.shape
    begin = grid.gc_index * own_rows
    padded = jnp.zeros((order + own_rows, order), jnp.float32)
    padded = lax.dynamic_update_slice_in_dim(padded, panel_block, jnp.minimum(begin, order), axis=0)
    out = []
    for a, b in grid.plane:
        start = ((grid.y ^ b) * grid.xs + (grid.x ^ a)) * chip_rows
        rows = masked_rows(rows_of(window, start, chip_rows), first_block, start)
        entries = rows_of(padded, start, chip_rows)
        high = lax.reduce_precision(entries, 8, 7)
        parts = [rows, high.astype(rows.dtype), (entries - high).astype(rows.dtype)]
        out.append(jnp.concatenate(parts, axis=1))
    return [jnp.where(grid.gr_index == 0, pack, jnp.zeros_like(pack)) for pack in out]


def panel_kernel(xs, ys, cores, *refs):
    count = cores * xs * ys
    shards, packs, (panel_ref, total_ref) = refs[:count], refs[count:-2], refs[-2:]
    depth, width = shards[0].shape
    order = total_ref.shape[1]
    gr = lax.axis_index("gr")
    x, core = gr // cores, gr % cores
    for e in range(cores):
        for b in range(ys):
            for a in range(xs):
                place = jnp.bitwise_xor(x, a) * cores + jnp.bitwise_xor(core, e)
                columns = pl.ds(pl.multiple_of(place * width, width), width)
                panel_ref[b * depth : (b + 1) * depth, columns] = shards[(e * ys + b) * xs + a][...]
    total = jnp.zeros(total_ref.shape, jnp.float32)
    for b in range(ys):
        rows = packs[b * xs][:, :depth]
        for a in range(1, xs):
            rows = rows + packs[b * xs + a][:, :depth]
        total = total - jnp.dot(rows, panel_ref[b * depth : (b + 1) * depth, :], preferred_element_type=jnp.float32)
    for pack in packs:
        total = total + pack[:, depth : depth + order].astype(jnp.float32) + pack[:, depth + order :].astype(jnp.float32)
    total_ref[...] = total


def panel_and_pivot(grid, shards, packs):
    depth, width = shards[0].shape
    order = grid.gr * width
    return pl.pallas_call(
        functools.partial(panel_kernel, grid.xs, grid.ys, grid.cores),
        in_specs=[VMEM] * (len(shards) + len(packs)),
        out_specs=[VMEM, VMEM],
        out_shape=[shape(grid.ys * depth, order, shards[0].dtype), shape(packs[0].shape[0], order, jnp.float32)],
        compiler_params=PARAMS,
        cost_estimate=QUICK,
        name="panel_and_pivot",
    )(*placed(pltpu.VMEM, *shards, *packs))


def plain_panel_and_pivot(grid, shards, packs):
    depth = shards[0].shape[0]
    stack = jnp.stack(shards).reshape((grid.cores, grid.ys, grid.xs) + shards[0].shape)
    total, bands = 0.0, []
    for b in range(grid.ys):
        blocks = [stack[grid.core ^ (gr % grid.cores), b, grid.x ^ (gr // grid.cores)] for gr in range(grid.gr)]
        bands.append(jnp.concatenate(blocks, axis=1))
        rows = sum(pack[:, :depth] for pack in packs[b * grid.xs : (b + 1) * grid.xs])
        total = total - jnp.dot(rows, bands[b], preferred_element_type=jnp.float32)
    for pack in packs:
        high, low = jnp.split(pack[:, depth:].astype(jnp.float32), 2, axis=1)
        total = total + (high + low)
    return jnp.concatenate(bands, axis=0), total


def two_parts(value):
    high = value.astype(jnp.bfloat16)
    return high, (value - high.astype(jnp.float32)).astype(jnp.bfloat16)


def product(left, right):
    dot = functools.partial(jnp.dot, preferred_element_type=jnp.float32)
    return dot(left[0], right[0]) + (dot(left[0], right[1]) + dot(left[1], right[0]))


def inverse_kernel(xs, ys, cores, *refs):
    pieces, (high_ref, low_ref, scale_ref, pivot_ref) = refs[:-4], refs[-4:]
    piece = pieces[0].shape[0]
    gr, y = lax.axis_index("gr"), lax.axis_index("gc") % ys
    x, core = gr // cores, gr % cores
    for i, piece_ref in enumerate(pieces):
        e, n = divmod(i, xs * ys)
        chip = jnp.bitwise_xor(y, n // xs) * xs + jnp.bitwise_xor(x, n % xs)
        start = (chip * cores + jnp.bitwise_xor(core, e)) * piece
        pivot_ref[pl.ds(pl.multiple_of(start, piece), piece), :] = piece_ref[...]
    order = pivot_ref.shape[0]
    square = (order, order)
    diagonal = lax.broadcasted_iota(jnp.int32, square, 0) == lax.broadcasted_iota(jnp.int32, square, 1)
    pivot = pivot_ref[...]
    scale = jnp.sum(jnp.where(diagonal, pivot, 0.0)) / order
    power = jnp.where(diagonal, 1.0, 0.0) - pivot / scale
    rest = power
    parts = two_parts(power)
    for step in range(NS_ITERS - 1):
        power = product(parts, parts)
        parts = two_parts(power)
        rest = rest + power + product(two_parts(rest), parts)
    high_ref[...], low_ref[...] = two_parts(rest)
    scale_ref[0] = scale


def inverse_rest(grid, pieces):
    order = pieces[0].shape[1]
    half = shape(order, order, jnp.bfloat16)
    return pl.pallas_call(
        functools.partial(inverse_kernel, grid.xs, grid.ys, grid.cores),
        in_specs=[VMEM] * len(pieces),
        out_specs=[VMEM, VMEM, SMEM],
        out_shape=[half, half, jax.ShapeDtypeStruct((1,), jnp.float32)],
        scratch_shapes=[pltpu.VMEM((order, order), jnp.float32)],
        compiler_params=PARAMS,
        cost_estimate=QUICK,
        name="pivot_inverse",
    )(*placed(pltpu.VMEM, *pieces))


def factor_kernel(schur_ref, high_ref, low_ref, out_ref):
    rows, order = out_ref.shape
    schur = schur_ref[...]
    rest = high_ref[...], low_ref[...]
    out_ref[...] = schur + product(two_parts(schur), rest)
    start = (lax.axis_index("gr") * lax.axis_size("gc") + lax.axis_index("gc")) * rows

    @pl.when(start < order)
    def _():
        here = start + lax.broadcasted_iota(jnp.int32, (rows, order), 0)
        across = lax.broadcasted_iota(jnp.int32, (rows, order), 1)
        pick = jnp.where(here == across, 1.0, 0.0).astype(jnp.bfloat16)
        dot = functools.partial(jnp.dot, preferred_element_type=jnp.float32)
        inverse = pick.astype(jnp.float32) + (dot(pick, rest[0]) + dot(pick, rest[1]))
        out_ref[...] = jnp.where(here < order, inverse, out_ref[...])


def factor_rows(schur, high, low):
    rows, order = schur.shape
    return pl.pallas_call(
        factor_kernel,
        in_specs=[VMEM, VMEM, VMEM],
        out_specs=VMEM,
        out_shape=jax.ShapeDtypeStruct((rows, order), jnp.float32),
        compiler_params=PARAMS,
        cost_estimate=QUICK,
        name="factor_rows",
    )(*placed(pltpu.VMEM, schur, high, low))


def masked_rows(part, first_block, first_row):
    col_first = jnp.repeat(first_block, BLK)
    row_ids = first_row + jnp.arange(part.shape[0], dtype=jnp.int32)
    inside = (row_ids // BLK)[:, None] >= col_first[None, :]
    return jnp.where(inside, part, jnp.zeros_like(part))


def body(factor_window, upper_panel, panel_block, first_block):
    grid = Grid()
    local_rows, depth = factor_window.shape
    own_rows, panel_width = panel_block.shape
    chip_rows = panel_width // (grid.xs * grid.ys)
    whole_tiles = upper_panel.shape[1] % LANES == 0 and chip_rows % ROW_TILE == 0

    order = list(range(grid.zs - 1, -1, -1))
    chunks = masked_chunks if own_rows % ROW_TILE == 0 else plain_masked_chunks
    chunks = functools.partial(chunks, grid, factor_window, first_block)
    columns = {k: [None] * grid.ys for k in order}
    shards = {(0, 0): upper_panel}
    for b in range(1, grid.ys):
        got = grid.swap(chunks(order[:1], b, own_rows, upper_panel), dy=b)
        columns[order[0]][b] = got[:own_rows]
        shards[0, b] = jnp.concatenate(jnp.split(got[own_rows:], depth // upper_panel.shape[1], axis=1), axis=0)
    columns[order[0]][0] = chunks(order[:1], 0, own_rows)
    for b in range(grid.ys if order[1:] else 0):
        band = chunks(order[1:], b, own_rows)
        band = grid.swap(band, dy=b) if b else band
        for n, k in enumerate(order[1:]):
            columns[k][b] = band[n * own_rows : (n + 1) * own_rows]

    shards.update({(a, b): grid.swap(upper_panel, dx=a, dy=b) for a, b in grid.plane if a})
    shards = [shards[place] for place in grid.plane]
    if grid.cores > 1:
        shards = shards + [grid.swap(shard, dcore=1) for shard in shards]

    packs = (pivot_pack if whole_tiles else plain_pivot_pack)(grid, factor_window, panel_block, first_block, chip_rows)
    packs = [packs[0]] + [
        grid.permute(pack, lambda core: (0, 0, 1, 0) if core and grid.zs > 1 else (a, 0, 0, b))
        for pack, (a, b) in zip(packs[1:], grid.plane[1:])
    ]
    panel, total = (panel_and_pivot if whole_tiles else plain_panel_and_pivot)(grid, shards, packs)

    if grid.cores > 1:
        piece = chip_rows // grid.cores
        total = jnp.where(grid.core == 0, total[:piece], grid.swap(total[piece:], dcore=1))
    step = 1
    while step < grid.zs:
        total = total + grid.swap(total, dz=step)
        step *= 2
    pieces = [total] + [grid.swap(total, dx=a, dy=b) for a, b in grid.plane[1:]]
    if grid.cores > 1:
        pieces = pieces + [grid.swap(piece, dcore=1) for piece in pieces]
    high, low, scale = inverse_rest(grid, pieces)

    sums = {}
    for k in order:
        bands = [panel[j * depth : (j + 1) * depth] for j in range(grid.ys)]
        parts = [jnp.dot(part, band, preferred_element_type=jnp.float32) for part, band in zip(columns[k], bands)]
        sums[k] = sum(parts[1:], parts[0])
    step = 1
    while step < grid.zs:
        for k in sorted((k for k in sums if k & step), reverse=True):
            got = grid.swap(sums.pop(k).astype(WIRE), dz=step)
            sums[k ^ step] = sums[k ^ step] + got.astype(jnp.float32)
        step *= 2
    return factor_rows((panel_block - sums[0]) / scale[0], high, low)


def solution(mesh):
    return jax.shard_map(
        body,
        mesh=mesh,
        in_specs=(P("gr", "gc"), P("gc", "gr"), P(("gr", "gc"), None), P("gc")),
        out_specs=P(("gr", "gc"), None),
        check_vma=False,
    )
```

```python
import functools

import jax
import jax.numpy as jnp
from jax import lax
from jax.experimental import pallas as pl
from jax.experimental.pallas import tpu as pltpu
from jax.sharding import PartitionSpec as P

BLK = 128
NS_ITERS = 3
CORES = 2
WIRE = jnp.float16
LANES = 128
ROW_TILE = 16
VMEM = pl.BlockSpec(memory_space=pltpu.VMEM)
SMEM = pl.BlockSpec(memory_space=pltpu.SMEM)
HBM = pl.BlockSpec(memory_space=pltpu.HBM)
ANY = pl.BlockSpec(memory_space=pl.ANY)
QUICK = pl.CostEstimate(flops=0, bytes_accessed=0, transcendentals=0)
PARAMS = pltpu.CompilerParams(vmem_limit_bytes=12 * 2**20)


def inner_size(n):
    return max(d for d in range(1, n + 1) if n % d == 0 and d * d <= n)


class Grid:
    def __init__(self):
        self.gr = lax.axis_size("gr")
        self.gc = lax.axis_size("gc")
        self.cores = CORES if self.gr % CORES == 0 else 1
        self.xs = self.gr // self.cores
        self.ys = inner_size(self.gc)
        self.ps = 2 if self.gc // self.ys % 2 == 0 else 1
        self.qs = self.gc // self.ps
        self.gr_index, self.gc_index = lax.axis_index("gr"), lax.axis_index("gc")
        self.x, self.core = self.gr_index // self.cores, self.gr_index % self.cores
        self.p = pair_place(self.gc_index, self.ys, self.ps)
        self.plane = [(a, b) for b in range(self.ps) for a in range(self.xs)]

    def swap(self, value, dx=0, dcore=0, dp=0, dq=0):
        return self.permute(value, lambda core: (dx, dcore, dp, dq))

    def permute(self, value, moves):
        pairs = []
        for gr in range(self.gr):
            for gc in range(self.gc):
                core = gr % self.cores
                dx, dcore, dp, dq = moves(core)
                to_gr = ((gr // self.cores) ^ dx) * self.cores + (core ^ dcore)
                pairs.append((gr * self.gc + gc, to_gr * self.gc + partner(gc, self.ys, self.ps, dq, dp)))
        return lax.ppermute(value, ("gr", "gc"), pairs)


def pair_place(gc, ys, ps):
    return gc // ys % ps


def partner(gc, ys, ps, dq, dp):
    return (gc // ys ^ (dq // ys * ps) ^ dp) * ys + (gc % ys ^ dq % ys)


def rows_of(value, start, count):
    return lax.dynamic_slice_in_dim(value, start, count, axis=0)


def shape(rows, columns, dtype):
    return pltpu.VMEM((rows, columns), dtype)


def after(value, *others):
    return pl.pallas_call(
        lambda *refs: None,
        in_specs=[ANY] * (1 + len(others)),
        out_specs=ANY,
        out_shape=jax.ShapeDtypeStruct(value.shape, value.dtype),
        input_output_aliases={0: 0},
        compiler_params=PARAMS,
        cost_estimate=QUICK,
        name="after",
    )(value, *others)


def placed(space, *values):
    return [pltpu.with_memory_space_constraint(value, space) for value in values]


def below_skyline(part, first_row, first_of):
    row_ids = first_row + lax.broadcasted_iota(jnp.int32, (part.shape[0], 1), 0)
    kept = []
    for c in range(part.shape[1] // BLK):
        block = part[:, c * BLK : (c + 1) * BLK]
        kept.append(jnp.where(row_ids >= first_of(c) * BLK, block, jnp.zeros_like(block)))
    return jnp.concatenate(kept, axis=1)


def across(shard, columns):
    return jnp.concatenate(jnp.split(shard, columns // shard.shape[1], axis=0), axis=1)


def chunks_kernel(ys, ps, wanted, own_rows, shards, first_ref, window_ref, *refs):
    shard_refs, refs = refs[:shards], refs[shards:]
    out_refs, (first, first_sem, sems) = refs[: len(wanted)], refs[len(wanted) : len(wanted) + 3]
    gr, gc = lax.axis_index("gr"), lax.axis_index("gc")
    first_copy = pltpu.make_async_copy(first_ref, first, first_sem)
    first_copy.start()
    copies = []
    for out_ref, chunks in zip(out_refs, wanted):
        for n, (k, j) in enumerate(chunks):
            start = partner(gc, ys, ps, k, j) * own_rows
            source = window_ref.at[pl.ds(pl.multiple_of(start, ROW_TILE), own_rows), :]
            place = out_ref.at[n * own_rows : (n + 1) * own_rows, :]
            copies.append((pltpu.make_async_copy(source, place, sems.at[len(copies)]), place, start))
            copies[-1][0].start()
    if shards:
        held, held_sem = refs[-2:]
        held_copy = pltpu.make_async_copy(shard_refs[0], held, held_sem)
        held_copy.start()
        held_copy.wait()
        out_refs[0][len(wanted[0]) * own_rows :, :] = across(held[...], out_refs[0].shape[1])
    first_copy.wait()
    for copy, place, start in copies:
        copy.wait()
        place[...] = below_skyline(place[...], gr * window_ref.shape[0] + start, lambda c: first[c])


def masked_chunks(grid, window, first_block, wanted, own_rows, *shard):
    extra = sum(part.size // window.shape[1] for part in shard)
    rows = [len(chunks) * own_rows for chunks in wanted]
    rows[0] += extra
    scratch = [
        pltpu.SMEM(first_block.shape, first_block.dtype),
        pltpu.SemaphoreType.DMA,
        pltpu.SemaphoreType.DMA((sum(len(chunks) for chunks in wanted),)),
    ]
    for part in shard:
        scratch += [pltpu.VMEM(part.shape, part.dtype), pltpu.SemaphoreType.DMA]
    return pl.pallas_call(
        functools.partial(chunks_kernel, grid.ys, grid.ps, wanted, own_rows, len(shard)),
        in_specs=[HBM] * (2 + len(shard)),
        out_specs=[VMEM] * len(wanted),
        out_shape=[shape(count, window.shape[1], window.dtype) for count in rows],
        scratch_shapes=scratch,
        compiler_params=PARAMS,
        cost_estimate=QUICK,
        name="masked_chunks",
    )(*placed(pltpu.HBM, first_block, window, *shard))


def plain_masked_chunks(grid, window, first_block, wanted, own_rows, *shard):
    out = []
    for chunks in wanted:
        parts = []
        for k, j in chunks:
            start = partner(grid.gc_index, grid.ys, grid.ps, k, j) * own_rows
            part = rows_of(window, start, own_rows)
            parts.append(masked_rows(part, first_block, grid.gr_index * window.shape[0] + start))
        if not out:
            parts += [across(part, window.shape[1]) for part in shard]
        out.append(jnp.concatenate(parts, axis=0))
    return out


def pivot_pack_kernel(xs, ys, ps, cores, first, window_ref, block_ref, *refs):
    out_refs, (head, padded, head_sem, block_sem) = refs[:-4], refs[-4:]
    chip_rows = out_refs[0].shape[0]
    own_rows, order = block_ref.shape
    depth = head.shape[1]
    gr, gc = lax.axis_index("gr"), lax.axis_index("gc")
    x, p = gr // cores, pair_place(gc, ys, ps)
    begin = gc * own_rows
    head_copy = pltpu.make_async_copy(window_ref.at[pl.ds(0, order), :], head, head_sem)
    block_copy = pltpu.make_async_copy(block_ref, padded.at[pl.ds(chip_rows, own_rows), :], block_sem)
    holds = (gr == 0) & (begin < order)

    def start_of(n):
        return ((p ^ n // xs) * xs + (x ^ n % xs)) * chip_rows

    @pl.when(gr == 0)
    def _():
        head_copy.start()

    @pl.when(holds)
    def _():
        block_copy.start()

    for out_ref in out_refs:
        out_ref[...] = jnp.zeros_like(out_ref)

    @pl.when(gr == 0)
    def _():
        head_copy.wait()
        for n, out_ref in enumerate(out_refs):
            rows = head[pl.ds(pl.multiple_of(start_of(n), chip_rows), chip_rows), :]
            out_ref[:, :depth] = below_skyline(rows, start_of(n), lambda c: first[c])

    @pl.when(holds)
    def _():
        edge = jnp.zeros((chip_rows, order), jnp.float32)
        padded[:chip_rows, :] = edge
        padded[chip_rows + own_rows :, :] = edge
        block_copy.wait()
        for n, out_ref in enumerate(out_refs):
            place = jnp.clip(start_of(n) - begin + chip_rows, 0, chip_rows + own_rows)
            high, low = two_parts(padded[pl.ds(pl.multiple_of(place, 8), chip_rows), :])
            out_ref[:, depth : depth + order] = high
            out_ref[:, depth + order :] = low


def pivot_pack(grid, window, panel_block, first_block, chip_rows):
    own_rows, order = panel_block.shape
    depth = window.shape[1]
    targets = len(grid.plane)
    return pl.pallas_call(
        functools.partial(pivot_pack_kernel, grid.xs, grid.ys, grid.ps, grid.cores),
        in_specs=[SMEM, HBM, HBM],
        out_specs=[VMEM] * targets,
        out_shape=[shape(chip_rows, depth + 2 * order, window.dtype)] * targets,
        scratch_shapes=[
            pltpu.VMEM((order, depth), window.dtype),
            pltpu.VMEM((own_rows + 2 * chip_rows, order), jnp.float32),
            pltpu.SemaphoreType.DMA,
            pltpu.SemaphoreType.DMA,
        ],
        compiler_params=PARAMS,
        cost_estimate=pl.CostEstimate(flops=0, bytes_accessed=36 * 2**20, transcendentals=0),
        name="pivot_pack",
    )(first_block, *placed(pltpu.HBM, window, panel_block))


def plain_pivot_pack(grid, window, panel_block, first_block, chip_rows):
    own_rows, order = panel_block.shape
    begin = grid.gc_index * own_rows
    padded = jnp.zeros((order + own_rows, order), jnp.float32)
    padded = lax.dynamic_update_slice_in_dim(padded, panel_block, jnp.minimum(begin, order), axis=0)
    out = []
    for a, b in grid.plane:
        start = ((grid.p ^ b) * grid.xs + (grid.x ^ a)) * chip_rows
        rows = masked_rows(rows_of(window, start, chip_rows), first_block, start)
        entries = rows_of(padded, start, chip_rows)
        high = lax.reduce_precision(entries, 8, 7)
        parts = [rows, high.astype(rows.dtype), (entries - high).astype(rows.dtype)]
        out.append(jnp.concatenate(parts, axis=1))
    return [jnp.where(grid.gr_index == 0, pack, jnp.zeros_like(pack)) for pack in out]


def panel_kernel(xs, ps, cores, *refs):
    shards, (panel_ref, sem) = refs[:-2], refs[-2:]
    depth, width = shards[0].shape
    gr = lax.axis_index("gr")
    x, core = gr // cores, gr % cores

    def place(i):
        (e, b), a = divmod(i // xs, ps), i % xs
        column = ((x ^ a) * cores + (core ^ e)) * width
        return panel_ref.at[b * depth : (b + 1) * depth, pl.ds(pl.multiple_of(column, width), width)]

    copy = pltpu.make_async_copy(shards[0], place(0), sem)
    copy.start()
    for i, shard in enumerate(shards):
        if i:
            place(i)[...] = shard[...]
    copy.wait()


def panel_assemble(grid, shards):
    depth, width = shards[0].shape
    return pl.pallas_call(
        functools.partial(panel_kernel, grid.xs, grid.ps, grid.cores),
        in_specs=[HBM] + [VMEM] * (len(shards) - 1),
        out_specs=VMEM,
        out_shape=shape(grid.ps * depth, grid.gr * width, shards[0].dtype),
        scratch_shapes=[pltpu.SemaphoreType.DMA],
        compiler_params=PARAMS,
        cost_estimate=QUICK,
        name="panel_assemble",
    )(*placed(pltpu.HBM, shards[0]), *placed(pltpu.VMEM, *shards[1:]))


def plain_panel_assemble(grid, shards):
    stack = jnp.stack(shards).reshape((grid.cores, grid.ps, grid.xs) + shards[0].shape)
    bands = []
    for b in range(grid.ps):
        blocks = [stack[grid.core ^ (gr % grid.cores), b, grid.x ^ (gr // grid.cores)] for gr in range(grid.gr)]
        bands.append(jnp.concatenate(blocks, axis=1))
    return jnp.concatenate(bands, axis=0)


def pivot_kernel(xs, ps, panel_ref, *refs):
    packs, total_ref = refs[:-1], refs[-1]
    order = total_ref.shape[1]
    depth = panel_ref.shape[0] // ps
    total = jnp.zeros(total_ref.shape, jnp.float32)
    for b in range(ps):
        rows = packs[b * xs][:, :depth]
        for a in range(1, xs):
            rows = rows + packs[b * xs + a][:, :depth]
        total = total - jnp.dot(rows, panel_ref[b * depth : (b + 1) * depth, :], preferred_element_type=jnp.float32)
    for pack in packs:
        total = total + pack[:, depth : depth + order].astype(jnp.float32) + pack[:, depth + order :].astype(jnp.float32)
    total_ref[...] = total


def pivot_part(grid, panel, packs):
    return pl.pallas_call(
        functools.partial(pivot_kernel, grid.xs, grid.ps),
        in_specs=[VMEM] * (1 + len(packs)),
        out_specs=VMEM,
        out_shape=shape(packs[0].shape[0], panel.shape[1], jnp.float32),
        compiler_params=PARAMS,
        cost_estimate=QUICK,
        name="pivot_part",
    )(*placed(pltpu.VMEM, panel, *packs))


def two_parts(value):
    high = value.astype(jnp.bfloat16)
    return high, (value - high.astype(jnp.float32)).astype(jnp.bfloat16)


def product(left, right):
    dot = functools.partial(jnp.dot, preferred_element_type=jnp.float32)
    return dot(left[0], right[0]) + (dot(left[0], right[1]) + dot(left[1], right[0]))


def inverse_kernel(xs, ys, ps, cores, *refs):
    pieces, (high_ref, low_ref, scale_ref, pivot_ref) = refs[:-4], refs[-4:]
    piece = pieces[0].shape[0]
    gr, p = lax.axis_index("gr"), pair_place(lax.axis_index("gc"), ys, ps)
    x, core = gr // cores, gr % cores
    for i, piece_ref in enumerate(pieces):
        e, n = divmod(i, xs * ps)
        chip = (p ^ n // xs) * xs + (x ^ n % xs)
        start = (chip * cores + (core ^ e)) * piece
        pivot_ref[pl.ds(pl.multiple_of(start, piece), piece), :] = piece_ref[...]
    order = pivot_ref.shape[0]
    square = (order, order)
    diagonal = lax.broadcasted_iota(jnp.int32, square, 0) == lax.broadcasted_iota(jnp.int32, square, 1)
    pivot = pivot_ref[...]
    scale = jnp.sum(jnp.where(diagonal, pivot, 0.0)) / order
    power = jnp.where(diagonal, 1.0, 0.0) - pivot / scale
    rest = power
    parts = two_parts(power)
    for step in range(NS_ITERS - 1):
        power = product(parts, parts)
        parts = two_parts(power)
        rest = rest + power + product(two_parts(rest), parts)
    high_ref[:order, :], low_ref[:order, :] = two_parts(rest)
    scale_ref[0] = scale


def inverse_rest(grid, pieces, spare):
    order = pieces[0].shape[1]
    half = shape(order + spare, order, jnp.bfloat16)
    return pl.pallas_call(
        functools.partial(inverse_kernel, grid.xs, grid.ys, grid.ps, grid.cores),
        in_specs=[VMEM] * len(pieces),
        out_specs=[VMEM, VMEM, SMEM],
        out_shape=[half, half, jax.ShapeDtypeStruct((1,), jnp.float32)],
        scratch_shapes=[pltpu.VMEM((order, order), jnp.float32)],
        compiler_params=PARAMS,
        cost_estimate=QUICK,
        name="pivot_inverse",
    )(*placed(pltpu.VMEM, *pieces))


def factor_kernel(schur_ref, high_ref, low_ref, out_ref):
    rows, order = out_ref.shape
    schur = schur_ref[...]
    rest = high_ref[:order, :], low_ref[:order, :]
    out_ref[...] = schur + product(two_parts(schur), rest)
    start = (lax.axis_index("gr") * lax.axis_size("gc") + lax.axis_index("gc")) * rows

    @pl.when(start < order)
    def _():
        here = start + lax.broadcasted_iota(jnp.int32, (rows, order), 0)
        across = lax.broadcasted_iota(jnp.int32, (rows, order), 1)
        place = pl.ds(pl.multiple_of(start, ROW_TILE), rows)
        inverse = jnp.where(here == across, 1.0, 0.0) + high_ref[place, :].astype(jnp.float32)
        inverse = inverse + low_ref[place, :].astype(jnp.float32)
        out_ref[...] = jnp.where(here < order, inverse, out_ref[...])


def factor_rows(schur, high, low):
    rows, order = schur.shape
    return pl.pallas_call(
        factor_kernel,
        in_specs=[VMEM, VMEM, VMEM],
        out_specs=VMEM,
        out_shape=jax.ShapeDtypeStruct((rows, order), jnp.float32),
        compiler_params=PARAMS,
        cost_estimate=QUICK,
        name="factor_rows",
    )(*placed(pltpu.VMEM, schur, high, low))


def masked_rows(part, first_block, first_row):
    col_first = jnp.repeat(first_block, BLK)
    row_ids = first_row + jnp.arange(part.shape[0], dtype=jnp.int32)
    inside = (row_ids // BLK)[:, None] >= col_first[None, :]
    return jnp.where(inside, part, jnp.zeros_like(part))


def body(factor_window, upper_panel, panel_block, first_block):
    grid = Grid()
    local_rows, depth = factor_window.shape
    own_rows, panel_width = panel_block.shape
    chip_rows = panel_width // (grid.xs * grid.ps)
    whole_tiles = upper_panel.shape[1] % LANES == 0 and chip_rows % ROW_TILE == 0

    order = list(range(grid.qs - 1, -1, -1))
    chunks = masked_chunks if own_rows % ROW_TILE == 0 else plain_masked_chunks
    chunks = functools.partial(chunks, grid, factor_window, first_block)
    others = range(1, grid.ps)
    columns = {k: [None] * grid.ps for k in order}

    packs = list((pivot_pack if whole_tiles else plain_pivot_pack)(grid, factor_window, panel_block, first_block, chip_rows))
    token = packs[0]
    shards = {(0, 0): upper_panel}
    first = [[(order[0], b)] for b in others]
    first = chunks(first, own_rows, upper_panel)
    for b in others:
        got = grid.swap(first[b - 1], dp=b)
        columns[order[0]][b] = got[:own_rows]
        shards[0, b] = jnp.concatenate(jnp.split(got[own_rows:], depth // upper_panel.shape[1], axis=1), axis=0)
    shards.update({(a, b): grid.swap(upper_panel, dx=a, dp=b) for a, b in grid.plane if a})
    shards[0, 1 % grid.ps] = after(shards[0, 1 % grid.ps], token)
    shards = [shards[place] for place in grid.plane]
    if grid.cores > 1:
        shards = shards + [grid.swap(shard, dcore=1) for shard in shards]
    panel = (panel_assemble if whole_tiles else plain_panel_assemble)(grid, shards)
    groups = [order[1:]]
    wanted = [([(k, b) for k in ks], ks, b) for ks in groups for b in others]
    own = order
    bands = chunks([names for names, _, _ in wanted] + [[(k, 0) for k in own]], own_rows)
    for n, k in enumerate(own):
        columns[k][0] = bands[-1][n * own_rows : (n + 1) * own_rows]

    def update(k):
        halves = [panel[j * depth : (j + 1) * depth] for j in range(grid.ps)]
        parts = [jnp.dot(part, half, preferred_element_type=jnp.float32) for part, half in zip(columns[k], halves)]
        return sum(parts[1:], parts[0])

    leading = update(order[0]).astype(WIRE)

    if grid.cores > 1:
        piece = chip_rows // grid.cores
    packs = [packs[0]] + [
        grid.permute(pack, lambda core: (0, 0, 0, 1) if core and grid.qs > 1 else (a, 0, b, 0))
        for pack, (a, b) in zip(packs[1:], grid.plane[1:])
    ]
    total = pivot_part(grid, panel, packs)
    if grid.cores > 1:
        total = jnp.where(grid.core == 0, total[:piece], grid.swap(total[piece:], dcore=1))
    bands = [grid.swap(band, dp=b) for band, (_, _, b) in zip(bands, wanted)]

    def arrive(lists, total):
        for band, (_, ks, b) in lists:
            band = after(band, total) if total is not None else band
            for n, k in enumerate(ks):
                columns[k][b] = band[n * own_rows : (n + 1) * own_rows]

    step, sums, last = 1, {}, {}
    while step < grid.qs:
        got = grid.swap(total, dq=step)
        if step == 1:
            sending = {order[0]: grid.swap(leading, dq=1)}
            total = total + got
            arrive(zip(bands, wanted), total)
            sums = {k: update(k) for k in order[1:]}
            sending.update({k: grid.swap(sums.pop(k).astype(WIRE), dq=1) for k in order[1:] if k & 1 and k > 1})
            last = {k: sums.pop(k).astype(WIRE) for k in order[1:] if k == 1 and k in sums}
        else:
            ready = {k: sums.pop(k).astype(WIRE) for k in list(sums) if k & step}
            got = after(got, *(value[:8, :LANES].astype(jnp.float32) for value in (*ready.values(), *last.values())))
            total = total + got
            for k, value in last.items():
                sums[0] = sums[0] + grid.swap(value, dq=1).astype(jnp.float32)
            last = {}
            sending = {k: grid.swap(value, dq=step) for k, value in ready.items()}
        for k, value in sending.items():
            sums[k ^ step] = sums[k ^ step] + value.astype(jnp.float32)
        step *= 2

    pieces = [total] + [grid.swap(total, dx=a, dp=b) for a, b in grid.plane[1:]]
    if grid.cores > 1:
        pieces = pieces + [grid.swap(piece, dcore=1) for piece in pieces]
    high, low, scale = inverse_rest(grid, pieces, own_rows)
    return factor_rows((panel_block - sums[0]) / scale[0], high, low)


def solution(mesh):
    return jax.shard_map(
        body,
        mesh=mesh,
        in_specs=(P("gr", "gc"), P("gc", "gr"), P(("gr", "gc"), None), P("gc")),
        out_specs=P(("gr", "gc"), None),
        check_vma=False,
    )
```

```python
import functools

import jax
import jax.numpy as jnp
from jax import lax
from jax.experimental import pallas as pl
from jax.experimental.pallas import tpu as pltpu
from jax.sharding import PartitionSpec as P

BLK = 128
NS_ITERS = 3
CORES = 2
WIRE = jnp.float16
LANES = 128
ROW_TILE = 16
VMEM = pl.BlockSpec(memory_space=pltpu.VMEM)
SMEM = pl.BlockSpec(memory_space=pltpu.SMEM)
HBM = pl.BlockSpec(memory_space=pltpu.HBM)
ANY = pl.BlockSpec(memory_space=pl.ANY)
QUICK = pl.CostEstimate(flops=0, bytes_accessed=0, transcendentals=0)
PARAMS = pltpu.CompilerParams(vmem_limit_bytes=12 * 2**20)


def inner_size(n):
    return max(d for d in range(1, n + 1) if n % d == 0 and d * d <= n)


class Grid:
    def __init__(self):
        self.gr = lax.axis_size("gr")
        self.gc = lax.axis_size("gc")
        self.cores = CORES if self.gr % CORES == 0 else 1
        self.xs = self.gr // self.cores
        self.ys = inner_size(self.gc)
        self.ps = 2 if self.gc // self.ys % 2 == 0 else 1
        self.qs = self.gc // self.ps
        self.gr_index, self.gc_index = lax.axis_index("gr"), lax.axis_index("gc")
        self.x, self.core = self.gr_index // self.cores, self.gr_index % self.cores
        self.p = pair_place(self.gc_index, self.ys, self.ps)
        self.plane = [(a, b) for b in range(self.ps) for a in range(self.xs)]

    def swap(self, value, dx=0, dcore=0, dp=0, dq=0):
        return self.permute(value, lambda core: (dx, dcore, dp, dq))

    def permute(self, value, moves):
        pairs = []
        for gr in range(self.gr):
            for gc in range(self.gc):
                core = gr % self.cores
                dx, dcore, dp, dq = moves(core)
                to_gr = ((gr // self.cores) ^ dx) * self.cores + (core ^ dcore)
                pairs.append((gr * self.gc + gc, to_gr * self.gc + partner(gc, self.ys, self.ps, dq, dp)))
        return lax.ppermute(value, ("gr", "gc"), pairs)


def pair_place(gc, ys, ps):
    return gc // ys % ps


def partner(gc, ys, ps, dq, dp):
    return (gc // ys ^ (dq // ys * ps) ^ dp) * ys + (gc % ys ^ dq % ys)


def rows_of(value, start, count):
    return lax.dynamic_slice_in_dim(value, start, count, axis=0)


def shape(rows, columns, dtype):
    return pltpu.VMEM((rows, columns), dtype)


def after(value, *others):
    return pl.pallas_call(
        lambda *refs: None,
        in_specs=[ANY] * (1 + len(others)),
        out_specs=ANY,
        out_shape=jax.ShapeDtypeStruct(value.shape, value.dtype),
        input_output_aliases={0: 0},
        compiler_params=PARAMS,
        cost_estimate=QUICK,
        name="after",
    )(value, *others)


def placed(space, *values):
    return [pltpu.with_memory_space_constraint(value, space) for value in values]


def below_skyline(part, first_row, first_of):
    row_ids = first_row + lax.broadcasted_iota(jnp.int32, (part.shape[0], 1), 0)
    kept = []
    for c in range(part.shape[1] // BLK):
        block = part[:, c * BLK : (c + 1) * BLK]
        kept.append(jnp.where(row_ids >= first_of(c) * BLK, block, jnp.zeros_like(block)))
    return jnp.concatenate(kept, axis=1)


def across(shard, columns):
    return jnp.concatenate(jnp.split(shard, columns // shard.shape[1], axis=0), axis=1)


def chunks_kernel(ys, ps, wanted, own_rows, shards, first_ref, window_ref, *refs):
    shard_refs, refs = refs[:shards], refs[shards:]
    out_refs, (first, first_sem, sems) = refs[: len(wanted)], refs[len(wanted) : len(wanted) + 3]
    gr, gc = lax.axis_index("gr"), lax.axis_index("gc")
    first_copy = pltpu.make_async_copy(first_ref, first, first_sem)
    first_copy.start()
    copies = []
    for out_ref, chunks in zip(out_refs, wanted):
        for n, (k, j) in enumerate(chunks):
            start = partner(gc, ys, ps, k, j) * own_rows
            source = window_ref.at[pl.ds(pl.multiple_of(start, ROW_TILE), own_rows), :]
            place = out_ref.at[n * own_rows : (n + 1) * own_rows, :]
            copies.append((pltpu.make_async_copy(source, place, sems.at[len(copies)]), place, start))
            copies[-1][0].start()
    if shards:
        held, held_sem = refs[-2:]
        held_copy = pltpu.make_async_copy(shard_refs[0], held, held_sem)
        held_copy.start()
        held_copy.wait()
        out_refs[0][len(wanted[0]) * own_rows :, :] = across(held[...], out_refs[0].shape[1])
    first_copy.wait()
    for copy, place, start in copies:
        copy.wait()
        place[...] = below_skyline(place[...], gr * window_ref.shape[0] + start, lambda c: first[c])


def masked_chunks(grid, window, first_block, wanted, own_rows, *shard):
    extra = sum(part.size // window.shape[1] for part in shard)
    rows = [len(chunks) * own_rows for chunks in wanted]
    rows[0] += extra
    scratch = [
        pltpu.SMEM(first_block.shape, first_block.dtype),
        pltpu.SemaphoreType.DMA,
        pltpu.SemaphoreType.DMA((sum(len(chunks) for chunks in wanted),)),
    ]
    for part in shard:
        scratch += [pltpu.VMEM(part.shape, part.dtype), pltpu.SemaphoreType.DMA]
    return pl.pallas_call(
        functools.partial(chunks_kernel, grid.ys, grid.ps, wanted, own_rows, len(shard)),
        in_specs=[HBM] * (2 + len(shard)),
        out_specs=[VMEM] * len(wanted),
        out_shape=[shape(count, window.shape[1], window.dtype) for count in rows],
        scratch_shapes=scratch,
        compiler_params=PARAMS,
        cost_estimate=pl.CostEstimate(flops=0, bytes_accessed=36 * 2**20, transcendentals=0),
        name="masked_chunks",
    )(*placed(pltpu.HBM, first_block, window, *shard))


def plain_masked_chunks(grid, window, first_block, wanted, own_rows, *shard):
    out = []
    for chunks in wanted:
        parts = []
        for k, j in chunks:
            start = partner(grid.gc_index, grid.ys, grid.ps, k, j) * own_rows
            part = rows_of(window, start, own_rows)
            parts.append(masked_rows(part, first_block, grid.gr_index * window.shape[0] + start))
        if not out:
            parts += [across(part, window.shape[1]) for part in shard]
        out.append(jnp.concatenate(parts, axis=0))
    return out


def pivot_pack_kernel(xs, ys, ps, cores, first, window_ref, block_ref, *refs):
    out_refs, (head, padded, head_sem, block_sem) = refs[:-4], refs[-4:]
    chip_rows = out_refs[0].shape[0]
    own_rows, order = block_ref.shape
    depth = head.shape[1]
    gr, gc = lax.axis_index("gr"), lax.axis_index("gc")
    x, p = gr // cores, pair_place(gc, ys, ps)
    begin = gc * own_rows
    head_copy = pltpu.make_async_copy(window_ref.at[pl.ds(0, order), :], head, head_sem)
    block_copy = pltpu.make_async_copy(block_ref, padded.at[pl.ds(chip_rows, own_rows), :], block_sem)
    holds = (gr == 0) & (begin < order)

    def start_of(n):
        return ((p ^ n // xs) * xs + (x ^ n % xs)) * chip_rows

    @pl.when(gr == 0)
    def _():
        head_copy.start()

    @pl.when(holds)
    def _():
        block_copy.start()

    for out_ref in out_refs:
        out_ref[...] = jnp.zeros_like(out_ref)

    @pl.when(gr == 0)
    def _():
        head_copy.wait()
        for n, out_ref in enumerate(out_refs):
            rows = head[pl.ds(pl.multiple_of(start_of(n), chip_rows), chip_rows), :]
            out_ref[:, :depth] = below_skyline(rows, start_of(n), lambda c: first[c])

    @pl.when(holds)
    def _():
        edge = jnp.zeros((chip_rows, order), jnp.float32)
        padded[:chip_rows, :] = edge
        padded[chip_rows + own_rows :, :] = edge
        block_copy.wait()
        for n, out_ref in enumerate(out_refs):
            place = jnp.clip(start_of(n) - begin + chip_rows, 0, chip_rows + own_rows)
            high, low = two_parts(padded[pl.ds(pl.multiple_of(place, 8), chip_rows), :])
            out_ref[:, depth : depth + order] = high
            out_ref[:, depth + order :] = low


def pivot_pack(grid, window, panel_block, first_block, chip_rows):
    own_rows, order = panel_block.shape
    depth = window.shape[1]
    targets = len(grid.plane)
    return pl.pallas_call(
        functools.partial(pivot_pack_kernel, grid.xs, grid.ys, grid.ps, grid.cores),
        in_specs=[SMEM, HBM, HBM],
        out_specs=[VMEM] * targets,
        out_shape=[shape(chip_rows, depth + 2 * order, window.dtype)] * targets,
        scratch_shapes=[
            pltpu.VMEM((order, depth), window.dtype),
            pltpu.VMEM((own_rows + 2 * chip_rows, order), jnp.float32),
            pltpu.SemaphoreType.DMA,
            pltpu.SemaphoreType.DMA,
        ],
        compiler_params=PARAMS,
        cost_estimate=QUICK,
        name="pivot_pack",
    )(first_block, *placed(pltpu.HBM, window, panel_block))


def plain_pivot_pack(grid, window, panel_block, first_block, chip_rows):
    own_rows, order = panel_block.shape
    begin = grid.gc_index * own_rows
    padded = jnp.zeros((order + own_rows, order), jnp.float32)
    padded = lax.dynamic_update_slice_in_dim(padded, panel_block, jnp.minimum(begin, order), axis=0)
    out = []
    for a, b in grid.plane:
        start = ((grid.p ^ b) * grid.xs + (grid.x ^ a)) * chip_rows
        rows = masked_rows(rows_of(window, start, chip_rows), first_block, start)
        entries = rows_of(padded, start, chip_rows)
        high = lax.reduce_precision(entries, 8, 7)
        parts = [rows, high.astype(rows.dtype), (entries - high).astype(rows.dtype)]
        out.append(jnp.concatenate(parts, axis=1))
    return [jnp.where(grid.gr_index == 0, pack, jnp.zeros_like(pack)) for pack in out]


def panel_kernel(xs, ps, cores, *refs):
    shards, (panel_ref, sem) = refs[:-2], refs[-2:]
    depth, width = shards[0].shape
    gr = lax.axis_index("gr")
    x, core = gr // cores, gr % cores

    def place(i):
        (e, b), a = divmod(i // xs, ps), i % xs
        column = ((x ^ a) * cores + (core ^ e)) * width
        return panel_ref.at[b * depth : (b + 1) * depth, pl.ds(pl.multiple_of(column, width), width)]

    copy = pltpu.make_async_copy(shards[0], place(0), sem)
    copy.start()
    for i, shard in enumerate(shards):
        if i:
            place(i)[...] = shard[...]
    copy.wait()


def panel_assemble(grid, shards):
    depth, width = shards[0].shape
    return pl.pallas_call(
        functools.partial(panel_kernel, grid.xs, grid.ps, grid.cores),
        in_specs=[HBM] + [VMEM] * (len(shards) - 1),
        out_specs=VMEM,
        out_shape=shape(grid.ps * depth, grid.gr * width, shards[0].dtype),
        scratch_shapes=[pltpu.SemaphoreType.DMA],
        compiler_params=PARAMS,
        cost_estimate=QUICK,
        name="panel_assemble",
    )(*placed(pltpu.HBM, shards[0]), *placed(pltpu.VMEM, *shards[1:]))


def plain_panel_assemble(grid, shards):
    stack = jnp.stack(shards).reshape((grid.cores, grid.ps, grid.xs) + shards[0].shape)
    bands = []
    for b in range(grid.ps):
        blocks = [stack[grid.core ^ (gr % grid.cores), b, grid.x ^ (gr // grid.cores)] for gr in range(grid.gr)]
        bands.append(jnp.concatenate(blocks, axis=1))
    return jnp.concatenate(bands, axis=0)


def pivot_kernel(xs, ps, panel_ref, *refs):
    packs, total_ref = refs[:-1], refs[-1]
    order = total_ref.shape[1]
    depth = panel_ref.shape[0] // ps
    total = jnp.zeros(total_ref.shape, jnp.float32)
    for b in range(ps):
        rows = packs[b * xs][:, :depth]
        for a in range(1, xs):
            rows = rows + packs[b * xs + a][:, :depth]
        total = total - jnp.dot(rows, panel_ref[b * depth : (b + 1) * depth, :], preferred_element_type=jnp.float32)
    for pack in packs:
        total = total + pack[:, depth : depth + order].astype(jnp.float32) + pack[:, depth + order :].astype(jnp.float32)
    total_ref[...] = total


def pivot_part(grid, panel, packs):
    return pl.pallas_call(
        functools.partial(pivot_kernel, grid.xs, grid.ps),
        in_specs=[VMEM] * (1 + len(packs)),
        out_specs=VMEM,
        out_shape=shape(packs[0].shape[0], panel.shape[1], jnp.float32),
        compiler_params=PARAMS,
        cost_estimate=QUICK,
        name="pivot_part",
    )(*placed(pltpu.VMEM, panel, *packs))


def two_parts(value):
    high = value.astype(jnp.bfloat16)
    return high, (value - high.astype(jnp.float32)).astype(jnp.bfloat16)


def product(left, right):
    dot = functools.partial(jnp.dot, preferred_element_type=jnp.float32)
    return dot(left[0], right[0]) + (dot(left[0], right[1]) + dot(left[1], right[0]))


def inverse_kernel(xs, ys, ps, cores, *refs):
    pieces, (high_ref, low_ref, scale_ref, pivot_ref) = refs[:-4], refs[-4:]
    piece = pieces[0].shape[0]
    gr, p = lax.axis_index("gr"), pair_place(lax.axis_index("gc"), ys, ps)
    x, core = gr // cores, gr % cores
    for i, piece_ref in enumerate(pieces):
        e, n = divmod(i, xs * ps)
        chip = (p ^ n // xs) * xs + (x ^ n % xs)
        start = (chip * cores + (core ^ e)) * piece
        pivot_ref[pl.ds(pl.multiple_of(start, piece), piece), :] = piece_ref[...]
    order = pivot_ref.shape[0]
    square = (order, order)
    diagonal = lax.broadcasted_iota(jnp.int32, square, 0) == lax.broadcasted_iota(jnp.int32, square, 1)
    pivot = pivot_ref[...]
    scale = jnp.sum(jnp.where(diagonal, pivot, 0.0)) / order
    power = jnp.where(diagonal, 1.0, 0.0) - pivot / scale
    rest = power
    parts = two_parts(power)
    for step in range(NS_ITERS - 1):
        power = product(parts, parts)
        parts = two_parts(power)
        rest = rest + power + product(two_parts(rest), parts)
    high_ref[:order, :], low_ref[:order, :] = two_parts(rest)
    scale_ref[0] = scale


def inverse_rest(grid, pieces, spare):
    order = pieces[0].shape[1]
    half = shape(order + spare, order, jnp.bfloat16)
    return pl.pallas_call(
        functools.partial(inverse_kernel, grid.xs, grid.ys, grid.ps, grid.cores),
        in_specs=[VMEM] * len(pieces),
        out_specs=[VMEM, VMEM, SMEM],
        out_shape=[half, half, jax.ShapeDtypeStruct((1,), jnp.float32)],
        scratch_shapes=[pltpu.VMEM((order, order), jnp.float32)],
        compiler_params=PARAMS,
        cost_estimate=QUICK,
        name="pivot_inverse",
    )(*placed(pltpu.VMEM, *pieces))


def factor_kernel(schur_ref, high_ref, low_ref, out_ref):
    rows, order = out_ref.shape
    schur = schur_ref[...]
    rest = high_ref[:order, :], low_ref[:order, :]
    out_ref[...] = schur + product(two_parts(schur), rest)
    start = (lax.axis_index("gr") * lax.axis_size("gc") + lax.axis_index("gc")) * rows

    @pl.when(start < order)
    def _():
        here = start + lax.broadcasted_iota(jnp.int32, (rows, order), 0)
        across = lax.broadcasted_iota(jnp.int32, (rows, order), 1)
        place = pl.ds(pl.multiple_of(start, ROW_TILE), rows)
        inverse = jnp.where(here == across, 1.0, 0.0) + high_ref[place, :].astype(jnp.float32)
        inverse = inverse + low_ref[place, :].astype(jnp.float32)
        out_ref[...] = jnp.where(here < order, inverse, out_ref[...])


def factor_rows(schur, high, low):
    rows, order = schur.shape
    return pl.pallas_call(
        factor_kernel,
        in_specs=[VMEM, VMEM, VMEM],
        out_specs=VMEM,
        out_shape=jax.ShapeDtypeStruct((rows, order), jnp.float32),
        compiler_params=PARAMS,
        cost_estimate=QUICK,
        name="factor_rows",
    )(*placed(pltpu.VMEM, schur, high, low))


def masked_rows(part, first_block, first_row):
    col_first = jnp.repeat(first_block, BLK)
    row_ids = first_row + jnp.arange(part.shape[0], dtype=jnp.int32)
    inside = (row_ids // BLK)[:, None] >= col_first[None, :]
    return jnp.where(inside, part, jnp.zeros_like(part))


def body(factor_window, upper_panel, panel_block, first_block):
    grid = Grid()
    local_rows, depth = factor_window.shape
    own_rows, panel_width = panel_block.shape
    chip_rows = panel_width // (grid.xs * grid.ps)
    whole_tiles = upper_panel.shape[1] % LANES == 0 and chip_rows % ROW_TILE == 0

    order = list(range(grid.qs - 1, -1, -1))
    chunks = masked_chunks if own_rows % ROW_TILE == 0 else plain_masked_chunks
    chunks = functools.partial(chunks, grid, factor_window, first_block)
    others = range(1, grid.ps)
    columns = {k: [None] * grid.ps for k in order}

    packs = list((pivot_pack if whole_tiles else plain_pivot_pack)(grid, factor_window, panel_block, first_block, chip_rows))
    token = packs[0]
    shards = {(0, 0): upper_panel}
    first = [[(order[0], b)] for b in others]
    first = chunks(first, own_rows, upper_panel)
    for b in others:
        got = grid.swap(first[b - 1], dp=b)
        columns[order[0]][b] = got[:own_rows]
        shards[0, b] = jnp.concatenate(jnp.split(got[own_rows:], depth // upper_panel.shape[1], axis=1), axis=0)
    shards.update({(a, b): grid.swap(upper_panel, dx=a, dp=b) for a, b in grid.plane if a})
    shards[0, 1 % grid.ps] = after(shards[0, 1 % grid.ps], token)
    shards = [shards[place] for place in grid.plane]
    if grid.cores > 1:
        shards = shards + [grid.swap(shard, dcore=1) for shard in shards]
    panel = (panel_assemble if whole_tiles else plain_panel_assemble)(grid, shards)
    groups = [order[1:]]
    wanted = [([(k, b) for k in ks], ks, b) for ks in groups for b in others]
    own = order
    bands = chunks([names for names, _, _ in wanted] + [[(k, 0) for k in own]], own_rows)
    for n, k in enumerate(own):
        columns[k][0] = bands[-1][n * own_rows : (n + 1) * own_rows]

    def update(k):
        halves = [panel[j * depth : (j + 1) * depth] for j in range(grid.ps)]
        parts = [jnp.dot(part, half, preferred_element_type=jnp.float32) for part, half in zip(columns[k], halves)]
        return sum(parts[1:], parts[0])

    leading = update(order[0]).astype(WIRE)

    if grid.cores > 1:
        piece = chip_rows // grid.cores
    packs = [packs[0]] + [
        grid.permute(pack, lambda core: (0, 0, 0, 1) if core and grid.qs > 1 else (a, 0, b, 0))
        for pack, (a, b) in zip(packs[1:], grid.plane[1:])
    ]
    total = pivot_part(grid, panel, packs)
    if grid.cores > 1:
        total = jnp.where(grid.core == 0, total[:piece], grid.swap(total[piece:], dcore=1))
    bands = [grid.swap(band, dp=b) for band, (_, _, b) in zip(bands, wanted)]

    def arrive(lists, total):
        for band, (_, ks, b) in lists:
            band = after(band, total) if total is not None else band
            for n, k in enumerate(ks):
                columns[k][b] = band[n * own_rows : (n + 1) * own_rows]

    step, sums, last = 1, {}, {}
    while step < grid.qs:
        got = grid.swap(total, dq=step)
        if step == 1:
            sending = {order[0]: grid.swap(leading, dq=1)}
            total = total + got
            arrive(zip(bands, wanted), total)
            sums = {k: update(k) for k in order[1:]}
            sending.update({k: grid.swap(sums.pop(k).astype(WIRE), dq=1) for k in order[1:] if k & 1 and k > 1})
            last = {k: sums.pop(k).astype(WIRE) for k in order[1:] if k == 1 and k in sums}
        else:
            ready = {k: sums.pop(k).astype(WIRE) for k in list(sums) if k & step}
            got = after(got, *(value[:8, :LANES].astype(jnp.float32) for value in (*ready.values(), *last.values())))
            total = total + got
            for k, value in last.items():
                sums[0] = sums[0] + grid.swap(value, dq=1).astype(jnp.float32)
            last = {}
            sending = {k: grid.swap(value, dq=step) for k, value in ready.items()}
        if step * 2 >= grid.qs:
            break
        for k, value in sending.items():
            sums[k ^ step] = sums[k ^ step] + value.astype(jnp.float32)
        step *= 2
    base = after(panel_block - sums[0], total)

    pieces = [total] + [grid.swap(total, dx=a) for a in range(1, grid.xs)]
    later = after(total, pieces[-1])
    pieces = pieces + [grid.swap(later, dx=a, dp=b) for a, b in grid.plane if b]
    if grid.cores > 1:
        pieces = pieces + [grid.swap(piece, dcore=1) for piece in pieces]
    pieces[0] = after(pieces[0], base)
    high, low, scale = inverse_rest(grid, pieces, own_rows)
    schur_rows = base - sum(value.astype(jnp.float32) for value in sending.values())
    return factor_rows(schur_rows / scale[0], high, low)


def solution(mesh):
    return jax.shard_map(
        body,
        mesh=mesh,
        in_specs=(P("gr", "gc"), P("gc", "gr"), P(("gr", "gc"), None), P("gc")),
        out_specs=P(("gr", "gc"), None),
        check_vma=False,
    )
```

```python
import functools

import jax
import jax.numpy as jnp
from jax import lax
from jax.experimental import pallas as pl
from jax.experimental.pallas import tpu as pltpu
from jax.sharding import PartitionSpec as P

BLK = 128
NS_ITERS = 3
CORES = 2
WIRE = jnp.float16
LANES = 128
ROW_TILE = 16
VMEM = pl.BlockSpec(memory_space=pltpu.VMEM)
SMEM = pl.BlockSpec(memory_space=pltpu.SMEM)
HBM = pl.BlockSpec(memory_space=pltpu.HBM)
ANY = pl.BlockSpec(memory_space=pl.ANY)
QUICK = pl.CostEstimate(flops=0, bytes_accessed=0, transcendentals=0)
PARAMS = pltpu.CompilerParams(vmem_limit_bytes=12 * 2**20)


def inner_size(n):
    return max(d for d in range(1, n + 1) if n % d == 0 and d * d <= n)


class Grid:
    def __init__(self):
        self.gr = lax.axis_size("gr")
        self.gc = lax.axis_size("gc")
        self.cores = CORES if self.gr % CORES == 0 else 1
        self.xs = self.gr // self.cores
        self.ys = inner_size(self.gc)
        self.ps = 2 if self.gc // self.ys % 2 == 0 else 1
        self.qs = self.gc // self.ps
        self.gr_index, self.gc_index = lax.axis_index("gr"), lax.axis_index("gc")
        self.x, self.core = self.gr_index // self.cores, self.gr_index % self.cores
        self.p = pair_place(self.gc_index, self.ys, self.ps)
        self.plane = [(a, b) for b in range(self.ps) for a in range(self.xs)]

    def swap(self, value, dx=0, dcore=0, dp=0, dq=0):
        return self.permute(value, lambda core: (dx, dcore, dp, dq))

    def permute(self, value, moves):
        pairs = []
        for gr in range(self.gr):
            for gc in range(self.gc):
                core = gr % self.cores
                dx, dcore, dp, dq = moves(core)
                to_gr = ((gr // self.cores) ^ dx) * self.cores + (core ^ dcore)
                pairs.append((gr * self.gc + gc, to_gr * self.gc + partner(gc, self.ys, self.ps, dq, dp)))
        return lax.ppermute(value, ("gr", "gc"), pairs)


def pair_place(gc, ys, ps):
    return gc // ys % ps


def partner(gc, ys, ps, dq, dp):
    return (gc // ys ^ (dq // ys * ps) ^ dp) * ys + (gc % ys ^ dq % ys)


def rows_of(value, start, count):
    return lax.dynamic_slice_in_dim(value, start, count, axis=0)


def shape(rows, columns, dtype):
    return pltpu.VMEM((rows, columns), dtype)


def after(value, *others):
    return pl.pallas_call(
        lambda *refs: None,
        in_specs=[ANY] * (1 + len(others)),
        out_specs=ANY,
        out_shape=jax.ShapeDtypeStruct(value.shape, value.dtype),
        input_output_aliases={0: 0},
        compiler_params=PARAMS,
        cost_estimate=QUICK,
        name="after",
    )(value, *others)


def placed(space, *values):
    return [pltpu.with_memory_space_constraint(value, space) for value in values]


def below_skyline(part, first_row, first_of):
    row_ids = first_row + lax.broadcasted_iota(jnp.int32, (part.shape[0], 1), 0)
    kept = []
    for c in range(part.shape[1] // BLK):
        block = part[:, c * BLK : (c + 1) * BLK]
        kept.append(jnp.where(row_ids >= first_of(c) * BLK, block, jnp.zeros_like(block)))
    return jnp.concatenate(kept, axis=1)


def across(shard, columns):
    return jnp.concatenate(jnp.split(shard, columns // shard.shape[1], axis=0), axis=1)


def chunks_kernel(ys, ps, wanted, own_rows, shards, first_ref, window_ref, *refs):
    shard_refs, refs = refs[:shards], refs[shards:]
    out_refs, (first, first_sem, sems) = refs[: len(wanted)], refs[len(wanted) : len(wanted) + 3]
    gr, gc = lax.axis_index("gr"), lax.axis_index("gc")
    first_copy = pltpu.make_async_copy(first_ref, first, first_sem)
    first_copy.start()
    copies = []
    for out_ref, chunks in zip(out_refs, wanted):
        for n, (k, j) in enumerate(chunks):
            start = partner(gc, ys, ps, k, j) * own_rows
            source = window_ref.at[pl.ds(pl.multiple_of(start, ROW_TILE), own_rows), :]
            place = out_ref.at[n * own_rows : (n + 1) * own_rows, :]
            copies.append((pltpu.make_async_copy(source, place, sems.at[len(copies)]), place, start))
            copies[-1][0].start()
    if shards:
        held, held_sem = refs[-2:]
        held_copy = pltpu.make_async_copy(shard_refs[0], held, held_sem)
        held_copy.start()
        held_copy.wait()
        out_refs[0][len(wanted[0]) * own_rows :, :] = across(held[...], out_refs[0].shape[1])
    first_copy.wait()
    for copy, place, start in copies:
        copy.wait()
        place[...] = below_skyline(place[...], gr * window_ref.shape[0] + start, lambda c: first[c])


def masked_chunks(grid, window, first_block, wanted, own_rows, *shard):
    extra = sum(part.size // window.shape[1] for part in shard)
    rows = [len(chunks) * own_rows for chunks in wanted]
    rows[0] += extra
    scratch = [
        pltpu.SMEM(first_block.shape, first_block.dtype),
        pltpu.SemaphoreType.DMA,
        pltpu.SemaphoreType.DMA((sum(len(chunks) for chunks in wanted),)),
    ]
    for part in shard:
        scratch += [pltpu.VMEM(part.shape, part.dtype), pltpu.SemaphoreType.DMA]
    return pl.pallas_call(
        functools.partial(chunks_kernel, grid.ys, grid.ps, wanted, own_rows, len(shard)),
        in_specs=[HBM] * (2 + len(shard)),
        out_specs=[VMEM] * len(wanted),
        out_shape=[shape(count, window.shape[1], window.dtype) for count in rows],
        scratch_shapes=scratch,
        compiler_params=PARAMS,
        cost_estimate=pl.CostEstimate(flops=0, bytes_accessed=36 * 2**20, transcendentals=0),
        name="masked_chunks",
    )(*placed(pltpu.HBM, first_block, window, *shard))


def plain_masked_chunks(grid, window, first_block, wanted, own_rows, *shard):
    out = []
    for chunks in wanted:
        parts = []
        for k, j in chunks:
            start = partner(grid.gc_index, grid.ys, grid.ps, k, j) * own_rows
            part = rows_of(window, start, own_rows)
            parts.append(masked_rows(part, first_block, grid.gr_index * window.shape[0] + start))
        if not out:
            parts += [across(part, window.shape[1]) for part in shard]
        out.append(jnp.concatenate(parts, axis=0))
    return out


def pivot_pack_kernel(xs, ys, ps, cores, first, window_ref, block_ref, *refs):
    out_refs, (head, padded, head_sem, block_sem) = refs[:-4], refs[-4:]
    chip_rows = out_refs[0].shape[0]
    own_rows, order = block_ref.shape
    depth = head.shape[1]
    gr, gc = lax.axis_index("gr"), lax.axis_index("gc")
    x, p = gr // cores, pair_place(gc, ys, ps)
    begin = gc * own_rows
    head_copy = pltpu.make_async_copy(window_ref.at[pl.ds(0, order), :], head, head_sem)
    block_copy = pltpu.make_async_copy(block_ref, padded.at[pl.ds(chip_rows, own_rows), :], block_sem)
    holds = (gr == 0) & (begin < order)

    def start_of(n):
        return ((p ^ n // xs) * xs + (x ^ n % xs)) * chip_rows

    @pl.when(gr == 0)
    def _():
        head_copy.start()

    @pl.when(holds)
    def _():
        block_copy.start()

    for out_ref in out_refs:
        out_ref[...] = jnp.zeros_like(out_ref)

    @pl.when(gr == 0)
    def _():
        head_copy.wait()
        for n, out_ref in enumerate(out_refs):
            rows = head[pl.ds(pl.multiple_of(start_of(n), chip_rows), chip_rows), :]
            out_ref[:, :depth] = below_skyline(rows, start_of(n), lambda c: first[c])

    @pl.when(holds)
    def _():
        edge = jnp.zeros((chip_rows, order), jnp.float32)
        padded[:chip_rows, :] = edge
        padded[chip_rows + own_rows :, :] = edge
        block_copy.wait()
        for n, out_ref in enumerate(out_refs):
            place = jnp.clip(start_of(n) - begin + chip_rows, 0, chip_rows + own_rows)
            high, low = two_parts(padded[pl.ds(pl.multiple_of(place, 8), chip_rows), :])
            out_ref[:, depth : depth + order] = high
            out_ref[:, depth + order :] = low


def pivot_pack(grid, window, panel_block, first_block, chip_rows):
    own_rows, order = panel_block.shape
    depth = window.shape[1]
    targets = len(grid.plane)
    return pl.pallas_call(
        functools.partial(pivot_pack_kernel, grid.xs, grid.ys, grid.ps, grid.cores),
        in_specs=[SMEM, HBM, HBM],
        out_specs=[VMEM] * targets,
        out_shape=[shape(chip_rows, depth + 2 * order, window.dtype)] * targets,
        scratch_shapes=[
            pltpu.VMEM((order, depth), window.dtype),
            pltpu.VMEM((own_rows + 2 * chip_rows, order), jnp.float32),
            pltpu.SemaphoreType.DMA,
            pltpu.SemaphoreType.DMA,
        ],
        compiler_params=PARAMS,
        cost_estimate=QUICK,
        name="pivot_pack",
    )(first_block, *placed(pltpu.HBM, window, panel_block))


def plain_pivot_pack(grid, window, panel_block, first_block, chip_rows):
    own_rows, order = panel_block.shape
    begin = grid.gc_index * own_rows
    padded = jnp.zeros((order + own_rows, order), jnp.float32)
    padded = lax.dynamic_update_slice_in_dim(padded, panel_block, jnp.minimum(begin, order), axis=0)
    out = []
    for a, b in grid.plane:
        start = ((grid.p ^ b) * grid.xs + (grid.x ^ a)) * chip_rows
        rows = masked_rows(rows_of(window, start, chip_rows), first_block, start)
        entries = rows_of(padded, start, chip_rows)
        high = lax.reduce_precision(entries, 8, 7)
        parts = [rows, high.astype(rows.dtype), (entries - high).astype(rows.dtype)]
        out.append(jnp.concatenate(parts, axis=1))
    return [jnp.where(grid.gr_index == 0, pack, jnp.zeros_like(pack)) for pack in out]


def panel_kernel(xs, ps, cores, *refs):
    shards, (panel_ref, sem) = refs[:-2], refs[-2:]
    depth, width = shards[0].shape
    gr = lax.axis_index("gr")
    x, core = gr // cores, gr % cores

    def place(i):
        (e, b), a = divmod(i // xs, ps), i % xs
        column = ((x ^ a) * cores + (core ^ e)) * width
        return panel_ref.at[b * depth : (b + 1) * depth, pl.ds(pl.multiple_of(column, width), width)]

    copy = pltpu.make_async_copy(shards[0], place(0), sem)
    copy.start()
    for i, shard in enumerate(shards):
        if i:
            place(i)[...] = shard[...]
    copy.wait()


def panel_assemble(grid, shards):
    depth, width = shards[0].shape
    return pl.pallas_call(
        functools.partial(panel_kernel, grid.xs, grid.ps, grid.cores),
        in_specs=[HBM] + [VMEM] * (len(shards) - 1),
        out_specs=VMEM,
        out_shape=shape(grid.ps * depth, grid.gr * width, shards[0].dtype),
        scratch_shapes=[pltpu.SemaphoreType.DMA],
        compiler_params=PARAMS,
        cost_estimate=QUICK,
        name="panel_assemble",
    )(*placed(pltpu.HBM, shards[0]), *placed(pltpu.VMEM, *shards[1:]))


def plain_panel_assemble(grid, shards):
    stack = jnp.stack(shards).reshape((grid.cores, grid.ps, grid.xs) + shards[0].shape)
    bands = []
    for b in range(grid.ps):
        blocks = [stack[grid.core ^ (gr % grid.cores), b, grid.x ^ (gr // grid.cores)] for gr in range(grid.gr)]
        bands.append(jnp.concatenate(blocks, axis=1))
    return jnp.concatenate(bands, axis=0)


def pivot_kernel(xs, ps, panel_ref, *refs):
    packs, total_ref = refs[:-1], refs[-1]
    order = total_ref.shape[1]
    depth = panel_ref.shape[0] // ps
    total = jnp.zeros(total_ref.shape, jnp.float32)
    for b in range(ps):
        rows = packs[b * xs][:, :depth]
        for a in range(1, xs):
            rows = rows + packs[b * xs + a][:, :depth]
        total = total - jnp.dot(rows, panel_ref[b * depth : (b + 1) * depth, :], preferred_element_type=jnp.float32)
    for pack in packs:
        total = total + pack[:, depth : depth + order].astype(jnp.float32) + pack[:, depth + order :].astype(jnp.float32)
    total_ref[...] = total


def pivot_part(grid, panel, packs):
    return pl.pallas_call(
        functools.partial(pivot_kernel, grid.xs, grid.ps),
        in_specs=[VMEM] * (1 + len(packs)),
        out_specs=VMEM,
        out_shape=shape(packs[0].shape[0], panel.shape[1], jnp.float32),
        compiler_params=PARAMS,
        cost_estimate=QUICK,
        name="pivot_part",
    )(*placed(pltpu.VMEM, panel, *packs))


def two_parts(value):
    high = value.astype(jnp.bfloat16)
    return high, (value - high.astype(jnp.float32)).astype(jnp.bfloat16)


def product(left, right):
    dot = functools.partial(jnp.dot, preferred_element_type=jnp.float32)
    return dot(left[0], right[0]) + (dot(left[0], right[1]) + dot(left[1], right[0]))


def inverse_kernel(xs, ys, ps, cores, *refs):
    pieces, (high_ref, low_ref, scale_ref, pivot_ref) = refs[:-4], refs[-4:]
    piece = pieces[0].shape[0]
    gr, p = lax.axis_index("gr"), pair_place(lax.axis_index("gc"), ys, ps)
    x, core = gr // cores, gr % cores
    for i, piece_ref in enumerate(pieces):
        e, n = divmod(i, xs * ps)
        chip = (p ^ n // xs) * xs + (x ^ n % xs)
        start = (chip * cores + (core ^ e)) * piece
        pivot_ref[pl.ds(pl.multiple_of(start, piece), piece), :] = piece_ref[...]
    order = pivot_ref.shape[0]
    square = (order, order)
    diagonal = lax.broadcasted_iota(jnp.int32, square, 0) == lax.broadcasted_iota(jnp.int32, square, 1)
    pivot = pivot_ref[...]
    share = order / jnp.sum(jnp.where(diagonal, pivot, 0.0), keepdims=True)
    power = jnp.where(diagonal, 1.0, 0.0) - pivot * share
    rest = power
    parts = two_parts(power)
    for step in range(NS_ITERS - 1):
        power = product(parts, parts)
        parts = two_parts(power)
        rest = rest + power + product(two_parts(rest), parts)
    high_ref[:order, :], low_ref[:order, :] = two_parts(rest)
    scale_ref[0] = share[0, 0]


def inverse_rest(grid, pieces, spare):
    order = pieces[0].shape[1]
    half = shape(order + spare, order, jnp.bfloat16)
    return pl.pallas_call(
        functools.partial(inverse_kernel, grid.xs, grid.ys, grid.ps, grid.cores),
        in_specs=[VMEM] * len(pieces),
        out_specs=[VMEM, VMEM, SMEM],
        out_shape=[half, half, jax.ShapeDtypeStruct((1,), jnp.float32)],
        scratch_shapes=[pltpu.VMEM((order, order), jnp.float32)],
        compiler_params=PARAMS,
        cost_estimate=QUICK,
        name="pivot_inverse",
    )(*placed(pltpu.VMEM, *pieces))


def factor_kernel(schur_ref, high_ref, low_ref, out_ref):
    rows, order = out_ref.shape
    schur = schur_ref[...]
    rest = high_ref[:order, :], low_ref[:order, :]
    out_ref[...] = schur + product(two_parts(schur), rest)
    start = (lax.axis_index("gr") * lax.axis_size("gc") + lax.axis_index("gc")) * rows

    @pl.when(start < order)
    def _():
        here = start + lax.broadcasted_iota(jnp.int32, (rows, order), 0)
        across = lax.broadcasted_iota(jnp.int32, (rows, order), 1)
        place = pl.ds(pl.multiple_of(start, ROW_TILE), rows)
        inverse = jnp.where(here == across, 1.0, 0.0) + high_ref[place, :].astype(jnp.float32)
        inverse = inverse + low_ref[place, :].astype(jnp.float32)
        out_ref[...] = jnp.where(here < order, inverse, out_ref[...])


def factor_rows(schur, high, low):
    rows, order = schur.shape
    return pl.pallas_call(
        factor_kernel,
        in_specs=[VMEM, VMEM, VMEM],
        out_specs=VMEM,
        out_shape=jax.ShapeDtypeStruct((rows, order), jnp.float32),
        compiler_params=PARAMS,
        cost_estimate=QUICK,
        name="factor_rows",
    )(*placed(pltpu.VMEM, schur, high, low))


def masked_rows(part, first_block, first_row):
    col_first = jnp.repeat(first_block, BLK)
    row_ids = first_row + jnp.arange(part.shape[0], dtype=jnp.int32)
    inside = (row_ids // BLK)[:, None] >= col_first[None, :]
    return jnp.where(inside, part, jnp.zeros_like(part))


def body(factor_window, upper_panel, panel_block, first_block):
    grid = Grid()
    local_rows, depth = factor_window.shape
    own_rows, panel_width = panel_block.shape
    chip_rows = panel_width // (grid.xs * grid.ps)
    whole_tiles = upper_panel.shape[1] % LANES == 0 and chip_rows % ROW_TILE == 0

    order = list(range(grid.qs - 1, -1, -1))
    chunks = masked_chunks if own_rows % ROW_TILE == 0 else plain_masked_chunks
    chunks = functools.partial(chunks, grid, factor_window, first_block)
    others = range(1, grid.ps)
    columns = {k: [None] * grid.ps for k in order}

    packs = list((pivot_pack if whole_tiles else plain_pivot_pack)(grid, factor_window, panel_block, first_block, chip_rows))
    token = packs[0]
    shards = {(0, 0): upper_panel}
    first = [[(order[0], b)] for b in others]
    first = chunks(first, own_rows, upper_panel)
    for b in others:
        got = grid.swap(first[b - 1], dp=b)
        columns[order[0]][b] = got[:own_rows]
        shards[0, b] = jnp.concatenate(jnp.split(got[own_rows:], depth // upper_panel.shape[1], axis=1), axis=0)
    shards.update({(a, b): grid.swap(upper_panel, dx=a, dp=b) for a, b in grid.plane if a})
    shards[0, 1 % grid.ps] = after(shards[0, 1 % grid.ps], token)
    shards = [shards[place] for place in grid.plane]
    if grid.cores > 1:
        shards = shards + [grid.swap(shard, dcore=1) for shard in shards]
    panel = (panel_assemble if whole_tiles else plain_panel_assemble)(grid, shards)
    groups = [order[1:]]
    wanted = [([(k, b) for k in ks], ks, b) for ks in groups for b in others]
    own = order
    bands = chunks([names for names, _, _ in wanted] + [[(k, 0) for k in own]], own_rows)
    for n, k in enumerate(own):
        columns[k][0] = bands[-1][n * own_rows : (n + 1) * own_rows]

    def update(k):
        halves = [panel[j * depth : (j + 1) * depth] for j in range(grid.ps)]
        parts = [jnp.dot(part, half, preferred_element_type=jnp.float32) for part, half in zip(columns[k], halves)]
        return sum(parts[1:], parts[0])

    leading = update(order[0]).astype(WIRE)

    if grid.cores > 1:
        piece = chip_rows // grid.cores
    packs = [packs[0]] + [
        grid.permute(pack, lambda core: (0, 0, 0, 1) if core and grid.qs > 1 else (a, 0, b, 0))
        for pack, (a, b) in zip(packs[1:], grid.plane[1:])
    ]
    total = pivot_part(grid, panel, packs)
    if grid.cores > 1:
        total = jnp.where(grid.core == 0, total[:piece], grid.swap(total[piece:], dcore=1))
    bands = [grid.swap(band, dp=b) for band, (_, _, b) in zip(bands, wanted)]

    def arrive(lists, total):
        for band, (_, ks, b) in lists:
            band = after(band, total) if total is not None else band
            for n, k in enumerate(ks):
                columns[k][b] = band[n * own_rows : (n + 1) * own_rows]

    step, sums, last = 1, {}, {}
    while step < grid.qs:
        got = grid.swap(total, dq=step)
        if step == 1:
            sending = {order[0]: grid.swap(leading, dq=1)}
            total = total + got
            arrive(zip(bands, wanted), total)
            sums = {k: update(k) for k in order[1:]}
            sending.update({k: grid.swap(sums.pop(k).astype(WIRE), dq=1) for k in order[1:] if k & 1 and k > 1})
            last = {k: sums.pop(k).astype(WIRE) for k in order[1:] if k == 1 and k in sums}
        else:
            ready = {k: sums.pop(k).astype(WIRE) for k in list(sums) if k & step}
            got = after(got, *(value[:8, :LANES].astype(jnp.float32) for value in (*ready.values(), *last.values())))
            total = total + got
            for k, value in last.items():
                sums[0] = sums[0] + grid.swap(value, dq=1).astype(jnp.float32)
            last = {}
            sending = {k: grid.swap(value, dq=step) for k, value in ready.items()}
        if step * 2 >= grid.qs:
            break
        for k, value in sending.items():
            sums[k ^ step] = sums[k ^ step] + value.astype(jnp.float32)
        step *= 2
    base = after(panel_block - sums[0], total)

    pieces = [total] + [grid.swap(total, dx=a) for a in range(1, grid.xs)]
    later = after(total, pieces[-1])
    pieces = pieces + [grid.swap(later, dx=a, dp=b) for a, b in grid.plane if b]
    if grid.cores > 1:
        pieces = pieces + [grid.swap(piece, dcore=1) for piece in pieces]
    pieces[0] = after(pieces[0], base)
    high, low, share = inverse_rest(grid, pieces, own_rows)
    schur_rows = base - sum(value.astype(jnp.float32) for value in sending.values())
    return factor_rows(schur_rows * share[0], high, low)


def solution(mesh):
    return jax.shard_map(
        body,
        mesh=mesh,
        in_specs=(P("gr", "gc"), P("gc", "gr"), P(("gr", "gc"), None), P("gc")),
        out_specs=P(("gr", "gc"), None),
        check_vma=False,
    )
```
